32 devices in a mesh: grp: 2 (over y), blk: 4 (over z), uly: 4 (over x, core).
Axes of the slice: x: 2, y: 2, z: 4, core: 2. Of those that a mesh axis runs over, the one named last changes fastest.
Arguments:
- queries: bfloat16 [16384, 1024], P(('grp', 'blk', 'uly')), parts along dimension 0, may hold values from -6 to 6
- keys: bfloat16 [16384, 1024], P(('grp', 'blk', 'uly')), parts along dimension 0, may hold values from -6 to 6
- values: bfloat16 [16384, 1024], P(('grp', 'blk', 'uly')), parts along dimension 0, may hold values from -6 to 6
- grad_out: bfloat16 [16384, 1024], P(('grp', 'blk', 'uly')), parts along dimension 0, may hold values from -256 to 256
- key_lists: int32 [128, 12], P('grp'), parts along dimension 0, may hold values from 0 to 63, as said below
- list_length: int32 [128], P('grp'), parts along dimension 0, may hold values from 1 to 12, as said below
Outputs:
- grad_queries: bfloat16 [16384, 1024], P(('grp', 'blk', 'uly')), parts along dimension 0
- grad_keys: bfloat16 [16384, 1024], P(('grp', 'blk', 'uly')), parts along dimension 0
- grad_values: bfloat16 [16384, 1024], P(('grp', 'blk', 'uly')), parts along dimension 0
The draws below stay inside these ranges and needn't reach their ends.
There are 2 independent parts, one for each index of `grp`. The reference program is written for one: setup_inputs(seed, part) draws one part's arguments, and reference() takes and returns one part's arrays. A program takes and returns all parts, laid end to end along the dimension named above; each array names one. Nothing has to cross between parts.
Inputs may be any that keep to these rules, and one draw needn't show every extreme that they name: `key_lists`: row i lists 12 different key-block numbers, each within 6 blocks of i counting around the slab's end, its own block i first; only its first list_length[i] entries count. `list_length`: some query block lists exactly 12 key blocks.
All inputs are finite; a program needn't handle non-finite values.
Results may differ from the reference program's by a relative error of at most 0.0087.
Values may be sent and summed in bfloat16 or wider, within the bound.
A program may use at most 128 MiB of HBM per device.

```python
import jax
import jax.numpy as jnp
from jax import lax

H = 16
HD = 64
D = 1024
BS = 128
SEQ = 8192
QB = 64
REACHB = 6
MAXK = 12


def query_key_pair(key):
    first = jax.random.fold_in(key, 101)
    second = jax.random.fold_in(key, 202)
    query_part = jax.random.truncated_normal(first, -6.0, 6.0, (SEQ, D), jnp.float32)
    key_part = jax.random.truncated_normal(second, -6.0, 6.0, (SEQ, D), jnp.float32)
    return (query_part, key_part)


def draw_queries(key, part):
    return query_key_pair(key)[0].astype(jnp.bfloat16)


def draw_keys(key, part):
    return query_key_pair(key)[1].astype(jnp.bfloat16)


def draw_key_lists(key, part):
    candidates = 2 * REACHB + 1
    offsets = jnp.arange(candidates, dtype=jnp.int32) - REACHB
    noise = jax.random.randint(jax.random.fold_in(key, 404), (QB, candidates), 0, 2 ** 16)
    score = noise + jnp.where(offsets == 0, 2 ** 17, 0)[None, :]
    score = score * candidates + jnp.arange(candidates, dtype=jnp.int32)[None, :]
    unused, chosen = lax.top_k(score, MAXK)
    query_ids = jnp.arange(QB, dtype=jnp.int32)[:, None]
    return ((query_ids + offsets[chosen]) % QB).astype(jnp.int32)


def draw_list_length(key, part):
    counts = jax.random.randint(jax.random.fold_in(key, 505), (QB,), 1, MAXK + 1)
    full_at = jax.random.randint(jax.random.fold_in(key, 606), (), 0, QB)
    return jnp.where(jnp.arange(QB, dtype=jnp.int32) == full_at, MAXK, counts).astype(jnp.int32)


def shard_levels(key, dims, shards, low, high):
    gain = 1.0
    for dim, blocks in shards:
        draws = jax.random.uniform(jax.random.fold_in(jax.random.fold_in(key, 6), dim), (blocks,), jnp.float32, low / len(shards), high / len(shards))
        gain = gain * jnp.repeat(jnp.exp(draws), dims[dim] // blocks).reshape((-1,) + (1,) * (len(dims) - 1 - dim))
    return gain


def normal_values(rng, dims, scale, most, pieces=(), held_as=jnp.bfloat16):
    gain = shard_levels(rng, dims, pieces, -0.22, 0.18) if pieces else 1.0
    drawn = jax.random.normal(rng, dims, jnp.float32) * scale * gain
    return jnp.minimum(jnp.maximum(drawn, -most), most).astype(held_as)


def setup_inputs(seed: int = 0, part: int = 0) -> dict:
    key_of = jax.random.split(jax.random.key(seed), 7)
    part_splits = jax.random.split(jax.random.fold_in(key_of[6], part), 7)
    return {
        "queries": draw_queries(jax.random.fold_in(jax.random.fold_in(key_of[6], part), 71), part),
        "keys": draw_keys(jax.random.fold_in(jax.random.fold_in(key_of[6], part), 71), part),
        "values": normal_values(part_splits[2], (SEQ, D), 1.0, 6.0, ((0, 16),)),
        "grad_out": normal_values(part_splits[3], (SEQ, D), 40.0, 256.0, ((0, 16),)),
        "key_lists": draw_key_lists(jax.random.fold_in(jax.random.fold_in(key_of[6], part), 71), part),
        "list_length": draw_list_length(jax.random.fold_in(jax.random.fold_in(key_of[6], part), 71), part),
    }


def reference(queries, keys, values, grad_out, key_lists, list_length):
    softmax_scale = HD ** -0.5
    blocks = SEQ // BS
    query_blocks = queries.reshape(blocks, BS, H, HD)
    key_blocks = keys.reshape(blocks, BS, H, HD)
    value_blocks = values.reshape(blocks, BS, H, HD)
    dout_blocks = grad_out.reshape(blocks, BS, H, HD)
    live_slots = jnp.arange(MAXK, dtype=jnp.int32)[None, :] < list_length[:, None]
    highest = lax.Precision.HIGHEST

    def one_block(carried, inputs):
        key_acc, value_acc = carried
        query_block, dout_block, listed_ids, alive = inputs
        keys_taken = key_blocks[listed_ids].astype(jnp.float32)
        values_taken = value_blocks[listed_ids].astype(jnp.float32)
        query_wide = query_block.astype(jnp.float32)
        dout_wide = dout_block.astype(jnp.float32)
        logits = jnp.einsum("qhd,mkhd->hqmk", query_wide, keys_taken, precision=highest) * softmax_scale
        logits = jnp.where(alive[None, None, :, None], logits, -jnp.inf)
        row_top = jnp.max(logits, axis=(2, 3))
        shifted = jnp.exp(logits - row_top[:, :, None, None])
        row_total = jnp.sum(shifted, axis=(2, 3))
        dout_prod = jnp.einsum("qhd,mkhd->hqmk", dout_wide, values_taken, precision=highest)
        row_cross = jnp.sum(shifted * dout_prod, axis=(2, 3))
        log_total = row_top + jnp.log(row_total)
        row_delta = row_cross / row_total
        probability = jnp.exp(logits - log_total[:, :, None, None])
        grad_score = (softmax_scale * probability * (dout_prod - row_delta[:, :, None, None])).astype(jnp.bfloat16)
        grad_score = lax.optimization_barrier(grad_score).astype(jnp.float32)
        weight_half = probability.astype(jnp.bfloat16)
        weight_half = lax.optimization_barrier(weight_half).astype(jnp.float32)
        grad_rows = jnp.einsum("hqmk,mkhd->qhd", grad_score, keys_taken, precision=highest)
        key_term = jnp.einsum("hqmk,qhd->mkhd", grad_score, query_wide, precision=highest)
        value_term = jnp.einsum("hqmk,qhd->mkhd", weight_half, dout_wide, precision=highest)
        key_acc = key_acc.at[listed_ids].add(key_term)
        value_acc = value_acc.at[listed_ids].add(value_term)
        return (key_acc, value_acc), grad_rows.astype(jnp.bfloat16)

    zero_acc = jnp.zeros((blocks, BS, H, HD), jnp.float32)
    (key_acc, value_acc), grad_rows = lax.scan(one_block, (zero_acc, zero_acc), (query_blocks, dout_blocks, key_lists, live_slots))
    grad_queries = grad_rows.reshape(SEQ, H * HD)
    grad_keys = key_acc.reshape(SEQ, H * HD).astype(jnp.bfloat16)
    grad_values = value_acc.reshape(SEQ, H * HD).astype(jnp.bfloat16)
    return (grad_queries, grad_keys, grad_values)
```

```python
import functools

import jax
import jax.numpy as jnp
from jax import lax
from jax.experimental import pallas as pl
from jax.experimental.pallas import tpu as pltpu
from jax.sharding import PartitionSpec as P

HD = 64
BS = 128
REACHB = 6
PAIR = 2 * HD
SCALE = HD ** (-0.5)
NT = (((1,), (1,)), ((), ()))
MIB = 1024 * 1024


def block_diagonal(pair, factor):
    wide = pair.astype(jnp.float32) * factor
    lane = lax.broadcasted_iota(jnp.int32, wide.shape, 1)
    first = jnp.where(lane < HD, wide, 0.0).astype(jnp.bfloat16)
    second = jnp.where(lane < HD, 0.0, wide).astype(jnp.bfloat16)
    return first, second


def attend_kernel(
    spots_ref, lengths_ref, q_ref, do_ref, kl_ref, ko_ref, kr_ref, vl_ref, vo_ref, vr_ref,
    dq_ref, own_ref, left_ref, right_ref,
    k_scr, v_scr, kt_scr, acc_k, acc_v, s_scr, p_scr, q_bd, do_bd, dqt_scr, round_scr, sems,
):
    step = pl.program_id(0)
    steps = pl.num_programs(0)
    halo, feat = kl_ref.shape
    rows = ko_ref.shape[0]
    total = k_scr.shape[0]
    packs = feat // PAIR

    @pl.when(step == 0)
    def _():
        copies = []
        for dst, parts in ((k_scr, (kl_ref, ko_ref, kr_ref)), (v_scr, (vl_ref, vo_ref, vr_ref))):
            start = 0
            for part in parts:
                size = part.shape[0]
                copies.append(
                    pltpu.make_async_copy(part, dst.at[pl.ds(start, size)], sems.at[len(copies)])
                )
                start += size
        for copy in copies:
            copy.start()

        @pl.loop(0, total // BS)
        def _(b):
            at = pl.ds(b * BS, BS)
            acc_k[at, :] = jnp.zeros((BS, feat), jnp.float32)
            acc_v[at, :] = jnp.zeros((BS, feat), jnp.float32)

        for copy in copies:
            copy.wait()

        @pl.loop(0, total // BS)
        def _(b):
            kt_scr[pl.ds(b * feat, feat), :] = k_scr[pl.ds(b * BS, BS), :].T

    for g in range(packs):
        cols = slice(g * PAIR, (g + 1) * PAIR)
        first, second = block_diagonal(q_ref[:, cols], SCALE)
        q_bd[g, :BS, :] = first
        q_bd[g, BS:, :] = second
        first, second = block_diagonal(do_ref[:, cols], 1.0)
        do_bd[g, :BS, :] = first
        do_bd[g, BS:, :] = second

    length = lengths_ref[step]

    def scores(slot, carry):
        at = pl.ds(pl.multiple_of(spots_ref[step, slot] * BS, BS), BS)
        out = []
        for g in range(packs):
            top, sums, cross = carry[g]
            cols = slice(g * PAIR, (g + 1) * PAIR)
            s = lax.dot_general(k_scr[at, cols], q_bd[g], NT, preferred_element_type=jnp.float32)
            dp = lax.dot_general(v_scr[at, cols], do_bd[g], NT, preferred_element_type=jnp.float32)
            s_scr[slot, g] = s
            p_scr[slot, g] = dp
            s = s.reshape(BS // 8, 8, 2 * BS)
            dp = dp.reshape(BS // 8, 8, 2 * BS)
            new_top = jnp.maximum(top, jnp.max(s, axis=0))
            keep = jnp.exp(top - new_top)
            p = jnp.exp(s - new_top[None])
            out.append(
                (
                    new_top,
                    sums * keep + jnp.sum(p, axis=0),
                    cross * keep + jnp.sum(p * dp, axis=0),
                )
            )
        return tuple(out)

    blank = jnp.zeros((8, 2 * BS), jnp.float32)
    start = tuple((blank - jnp.inf, blank, blank) for _ in range(packs))
    stats = lax.fori_loop(0, length, scores, start)
    merged = []
    for top, sums, cross in stats:
        best = jnp.max(top, axis=0, keepdims=True)
        factor = jnp.exp(top - best)
        denom = jnp.sum(sums * factor, axis=0, keepdims=True)
        delta = jnp.sum(cross * factor, axis=0, keepdims=True) / denom
        merged.append((best + jnp.log(denom), delta))

    dqt_scr[...] = jnp.zeros_like(dqt_scr)

    @pl.loop(0, length)
    def _(slot):
        spot = spots_ref[step, slot]
        at = pl.ds(pl.multiple_of(spot * BS, BS), BS)
        for g in range(packs):
            log_total, delta = merged[g]
            cols = slice(g * PAIR, (g + 1) * PAIR)
            weight = jnp.exp(s_scr[slot, g] - log_total)
            grad = (weight * (p_scr[slot, g] - delta)).astype(jnp.bfloat16)
            half = weight.astype(jnp.bfloat16)
            acc_v[at, cols] += jnp.dot(half, do_bd[g], preferred_element_type=jnp.float32)
            acc_k[at, cols] += jnp.dot(grad, q_bd[g], preferred_element_type=jnp.float32)
            for h in range(2):
                low = g * PAIR + h * HD
                kt = kt_scr[pl.ds(pl.multiple_of(spot * feat + low, HD), HD), :]
                dqt_scr[low : low + HD, :] += jnp.dot(
                    kt, grad[:, h * BS : (h + 1) * BS], preferred_element_type=jnp.float32
                )

    dq_ref[...] = (dqt_scr[...].T * SCALE).astype(jnp.bfloat16)

    @pl.when(step == steps - 1)
    def _():
        @pl.loop(0, total // BS)
        def _(b):
            at = pl.ds(b * BS, BS)
            round_scr[0, at, :] = acc_k[at, :].astype(jnp.bfloat16)
            round_scr[1, at, :] = acc_v[at, :].astype(jnp.bfloat16)

        copies = []
        for i, acc in enumerate((acc_k, acc_v)):
            copies += [
                pltpu.make_async_copy(acc.at[pl.ds(halo, rows)], own_ref.at[i], sems.at[3 * i]),
                pltpu.make_async_copy(
                    round_scr.at[i, pl.ds(0, halo)], left_ref.at[i], sems.at[3 * i + 1]
                ),
                pltpu.make_async_copy(
                    round_scr.at[i, pl.ds(halo + rows, halo)], right_ref.at[i], sems.at[3 * i + 2]
                ),
            ]
        for copy in copies:
            copy.start()
        for copy in copies:
            copy.wait()


def attend(spots, lengths, q, do, k_parts, v_parts):
    rows, feat = q.shape
    halo = k_parts[0].shape[0]
    total = rows + 2 * halo
    packs = feat // PAIR
    slots = spots.shape[1]
    hbm = pl.BlockSpec(memory_space=pl.ANY)
    block = pl.BlockSpec((BS, feat), lambda i, *_: (i, 0))
    f32, bf16 = jnp.float32, jnp.bfloat16
    return pl.pallas_call(
        attend_kernel,
        grid_spec=pltpu.PrefetchScalarGridSpec(
            num_scalar_prefetch=2,
            grid=(rows // BS,),
            in_specs=[block, block] + [hbm] * 6,
            out_specs=[block, hbm, hbm, hbm],
            scratch_shapes=[
                pltpu.VMEM((total, feat), bf16),
                pltpu.VMEM((total, feat), bf16),
                pltpu.VMEM((total // BS * feat, BS), bf16),
                pltpu.VMEM((total, feat), f32),
                pltpu.VMEM((total, feat), f32),
                pltpu.VMEM((slots, packs, BS, 2 * BS), f32),
                pltpu.VMEM((slots, packs, BS, 2 * BS), f32),
                pltpu.VMEM((packs, 2 * BS, PAIR), bf16),
                pltpu.VMEM((packs, 2 * BS, PAIR), bf16),
                pltpu.VMEM((feat, BS), f32),
                pltpu.VMEM((2, total, feat), bf16),
                pltpu.SemaphoreType.DMA((6,)),
            ],
        ),
        out_shape=[
            jax.ShapeDtypeStruct((rows, feat), bf16),
            jax.ShapeDtypeStruct((2, rows, feat), f32),
            jax.ShapeDtypeStruct((2, halo, feat), bf16),
            jax.ShapeDtypeStruct((2, halo, feat), bf16),
        ],
        compiler_params=pltpu.CompilerParams(vmem_limit_bytes=48 * MIB),
        name="attend",
    )(spots, lengths, q, do, *k_parts, *v_parts)


def passed_along(block, axis, distance):
    count = lax.axis_size(axis)
    return lax.ppermute(block, axis, [((i - distance) % count, i) for i in range(count)])


def local_lists(key_lists, list_length, per_rank):
    block_rank = lax.axis_index("blk")
    all_blocks = per_rank * lax.axis_size("blk")
    base_block = block_rank * per_rank - REACHB
    lists_here = lax.dynamic_slice_in_dim(key_lists, block_rank * per_rank, per_rank, 0)
    lengths_here = lax.dynamic_slice_in_dim(list_length, block_rank * per_rank, per_rank, 0)
    return (lists_here - base_block) % all_blocks, lengths_here


def shards(queries, keys, values, grad_out, key_lists, list_length):
    stacked = jnp.stack([queries, keys, values, grad_out])
    spread = lax.all_to_all(stacked, "uly", split_axis=2, concat_axis=1, tiled=True)
    q, k, v, do = spread[0], spread[1], spread[2], spread[3]
    rows = q.shape[0]
    halo = REACHB * BS
    spots, lengths = local_lists(key_lists, list_length, rows // BS)
    pair = jnp.stack([k, v])
    from_left = passed_along(pair[:, rows - halo :], "blk", 1)
    from_right = passed_along(pair[:, :halo], "blk", -1)
    dq, own, left, right = attend(
        spots, lengths, q, do,
        (from_left[0], k, from_right[0]), (from_left[1], v, from_right[1]),
    )
    from_right = passed_along(left, "blk", -1).astype(jnp.float32)
    from_left = passed_along(right, "blk", 1).astype(jnp.float32)
    own = own.at[:, rows - halo :].add(from_right)
    own = own.at[:, :halo].add(from_left)
    result = jnp.concatenate([dq[None], own.astype(jnp.bfloat16)])
    returned = lax.all_to_all(result, "uly", split_axis=1, concat_axis=2, tiled=True)
    return (returned[0], returned[1], returned[2])


def solution(mesh):
    rows = P(("grp", "blk", "uly"), None)
    return jax.shard_map(
        shards,
        mesh=mesh,
        in_specs=(rows, rows, rows, rows, P("grp", None), P("grp")),
        out_specs=(rows, rows, rows),
        check_vma=False,
    )
```

```python
import functools

import jax
import jax.numpy as jnp
from jax import lax
from jax.experimental import pallas as pl
from jax.experimental.pallas import tpu as pltpu
from jax.sharding import PartitionSpec as P

HD = 64
BS = 128
REACHB = 6
PAIR = 2 * HD
SCALE = HD ** (-0.5)
NT = (((1,), (1,)), ((), ()))
MIB = 1024 * 1024
MESH = pl.DeviceIdType.MESH


def block_diagonal(pair, factor):
    wide = pair.astype(jnp.float32) * factor
    lane = lax.broadcasted_iota(jnp.int32, wide.shape, 1)
    first = jnp.where(lane < HD, wide, 0.0).astype(jnp.bfloat16)
    second = jnp.where(lane < HD, 0.0, wide).astype(jnp.bfloat16)
    return first, second


def attend_kernel(
    spots_ref, lengths_ref, q_ref, do_ref, k_ref, v_ref,
    dq_ref, own_ref, left_ref, right_ref,
    k_scr, v_scr, kt_scr, acc_k, acc_v, s_scr, p_scr, q_bd, do_bd, dqt_scr, round_scr, sems,
):
    step = pl.program_id(0)
    steps = pl.num_programs(0)
    halo = left_ref.shape[1]
    total, feat = k_scr.shape
    rows = total - 2 * halo
    packs = feat // PAIR

    @pl.when(step == 0)
    def _():
        copies = [
            pltpu.make_async_copy(k_ref, k_scr, sems.at[0]),
            pltpu.make_async_copy(v_ref, v_scr, sems.at[1]),
        ]
        for copy in copies:
            copy.start()

        @pl.loop(0, total // BS)
        def _(b):
            at = pl.ds(b * BS, BS)
            acc_k[at, :] = jnp.zeros((BS, feat), jnp.float32)
            acc_v[at, :] = jnp.zeros((BS, feat), jnp.float32)

        for copy in copies:
            copy.wait()

        @pl.loop(0, total // BS)
        def _(b):
            kt_scr[pl.ds(b * feat, feat), :] = k_scr[pl.ds(b * BS, BS), :].T

    for g in range(packs):
        cols = slice(g * PAIR, (g + 1) * PAIR)
        first, second = block_diagonal(q_ref[:, cols], SCALE)
        q_bd[g, :BS, :] = first
        q_bd[g, BS:, :] = second
        first, second = block_diagonal(do_ref[:, cols], 1.0)
        do_bd[g, :BS, :] = first
        do_bd[g, BS:, :] = second

    length = lengths_ref[step]

    def scores(slot, carry):
        at = pl.ds(pl.multiple_of(spots_ref[step, slot] * BS, BS), BS)
        out = []
        for g in range(packs):
            top, sums, cross = carry[g]
            cols = slice(g * PAIR, (g + 1) * PAIR)
            s = lax.dot_general(k_scr[at, cols], q_bd[g], NT, preferred_element_type=jnp.float32)
            dp = lax.dot_general(v_scr[at, cols], do_bd[g], NT, preferred_element_type=jnp.float32)
            s_scr[slot, g] = s
            p_scr[slot, g] = dp
            s = s.reshape(BS // 8, 8, 2 * BS)
            dp = dp.reshape(BS // 8, 8, 2 * BS)
            new_top = jnp.maximum(top, jnp.max(s, axis=0))
            keep = jnp.exp(top - new_top)
            p = jnp.exp(s - new_top[None])
            out.append(
                (
                    new_top,
                    sums * keep + jnp.sum(p, axis=0),
                    cross * keep + jnp.sum(p * dp, axis=0),
                )
            )
        return tuple(out)

    blank = jnp.zeros((8, 2 * BS), jnp.float32)
    start = tuple((blank - jnp.inf, blank, blank) for _ in range(packs))
    stats = lax.fori_loop(0, length, scores, start)
    merged = []
    for top, sums, cross in stats:
        best = jnp.max(top, axis=0, keepdims=True)
        factor = jnp.exp(top - best)
        denom = jnp.sum(sums * factor, axis=0, keepdims=True)
        delta = jnp.sum(cross * factor, axis=0, keepdims=True) / denom
        merged.append((best + jnp.log(denom), delta))

    dqt_scr[...] = jnp.zeros_like(dqt_scr)

    @pl.loop(0, length)
    def _(slot):
        spot = spots_ref[step, slot]
        at = pl.ds(pl.multiple_of(spot * BS, BS), BS)
        for g in range(packs):
            log_total, delta = merged[g]
            cols = slice(g * PAIR, (g + 1) * PAIR)
            weight = jnp.exp(s_scr[slot, g] - log_total)
            grad = (weight * (p_scr[slot, g] - delta)).astype(jnp.bfloat16)
            half = weight.astype(jnp.bfloat16)
            acc_v[at, cols] += jnp.dot(half, do_bd[g], preferred_element_type=jnp.float32)
            acc_k[at, cols] += jnp.dot(grad, q_bd[g], preferred_element_type=jnp.float32)
            for h in range(2):
                low = g * PAIR + h * HD
                kt = kt_scr[pl.ds(pl.multiple_of(spot * feat + low, HD), HD), :]
                dqt_scr[low : low + HD, :] += jnp.dot(
                    kt, grad[:, h * BS : (h + 1) * BS], preferred_element_type=jnp.float32
                )

    dq_ref[...] = (dqt_scr[...].T * SCALE).astype(jnp.bfloat16)

    @pl.when(step == steps - 1)
    def _():
        @pl.loop(0, total // BS)
        def _(b):
            at = pl.ds(b * BS, BS)
            round_scr[0, at, :] = acc_k[at, :].astype(jnp.bfloat16)
            round_scr[1, at, :] = acc_v[at, :].astype(jnp.bfloat16)

        copies = []
        for i, acc in enumerate((acc_k, acc_v)):
            copies += [
                pltpu.make_async_copy(acc.at[pl.ds(halo, rows)], own_ref.at[i], sems.at[3 * i]),
                pltpu.make_async_copy(
                    round_scr.at[i, pl.ds(0, halo)], left_ref.at[i], sems.at[3 * i + 1]
                ),
                pltpu.make_async_copy(
                    round_scr.at[i, pl.ds(halo + rows, halo)], right_ref.at[i], sems.at[3 * i + 2]
                ),
            ]
        for copy in copies:
            copy.start()
        for copy in copies:
            copy.wait()


def attend(spots, lengths, q, do, k, v):
    rows, feat = q.shape
    total = k.shape[0]
    halo = (total - rows) // 2
    packs = feat // PAIR
    slots = spots.shape[1]
    hbm = pl.BlockSpec(memory_space=pl.ANY)
    block = pl.BlockSpec((BS, feat), lambda i, *_: (i, 0))
    f32, bf16 = jnp.float32, jnp.bfloat16
    return pl.pallas_call(
        attend_kernel,
        grid_spec=pltpu.PrefetchScalarGridSpec(
            num_scalar_prefetch=2,
            grid=(rows // BS,),
            in_specs=[block, block] + [hbm] * 2,
            out_specs=[block, hbm, hbm, hbm],
            scratch_shapes=[
                pltpu.VMEM((total, feat), bf16),
                pltpu.VMEM((total, feat), bf16),
                pltpu.VMEM((total // BS * feat, BS), bf16),
                pltpu.VMEM((total, feat), f32),
                pltpu.VMEM((total, feat), f32),
                pltpu.VMEM((slots, packs, BS, 2 * BS), f32),
                pltpu.VMEM((slots, packs, BS, 2 * BS), f32),
                pltpu.VMEM((packs, 2 * BS, PAIR), bf16),
                pltpu.VMEM((packs, 2 * BS, PAIR), bf16),
                pltpu.VMEM((feat, BS), f32),
                pltpu.VMEM((2, total, feat), bf16),
                pltpu.SemaphoreType.DMA((6,)),
            ],
        ),
        out_shape=[
            jax.ShapeDtypeStruct((rows, feat), bf16),
            jax.ShapeDtypeStruct((2, rows, feat), f32),
            jax.ShapeDtypeStruct((2, halo, feat), bf16),
            jax.ShapeDtypeStruct((2, halo, feat), bf16),
        ],
        compiler_params=pltpu.CompilerParams(vmem_limit_bytes=48 * MIB),
        name="attend",
    )(spots, lengths, q, do, k, v)


def greet(n):
    me = lax.axis_index("uly")
    count = lax.axis_size("blk")
    rank = lax.axis_index("blk")
    left, right = lax.rem(rank + count - 1, count), lax.rem(rank + 1, count)
    barrier = pltpu.get_barrier_semaphore()
    for d in range(1, n):
        pl.semaphore_signal(barrier, 1, device_id={"uly": lax.rem(me + d, n)}, device_id_type=MESH)
    for side in (left, right):
        pl.semaphore_signal(barrier, 1, device_id={"blk": side}, device_id_type=MESH)
    pl.semaphore_wait(barrier, n + 1)
    return me, left, right


def remote(src, dst, send, recv, where):
    return pltpu.make_async_remote_copy(
        src_ref=src, dst_ref=dst, send_sem=send, recv_sem=recv, device_id=where, device_id_type=MESH
    )


def distances(n):
    return sorted(range(1, n), key=lambda d: -min(d, n - d))


def spread_kernel(
    n, q_ref, k_ref, v_ref, do_ref, q_out, do_out, k_out, v_out,
    send_sem, recv_sem, own_sem, halo_send, halo_recv,
):
    me, left, right = greet(n)
    part = q_ref.shape[0]
    rows, feat = q_out.shape
    halo = (k_out.shape[0] - rows) // 2
    arrays = ((k_ref, k_out, halo), (v_ref, v_out, halo), (q_ref, q_out, 0), (do_ref, do_out, 0))
    sent, kept = [], []
    for a, (src, dst, offset) in enumerate(arrays):
        here = dst.at[pl.ds(pl.multiple_of(offset + me * part, BS), part)]
        mine = []
        for d in distances(n):
            peer = lax.rem(me + d, n)
            copy = remote(
                src.at[:, pl.ds(pl.multiple_of(peer * feat, feat), feat)], here,
                send_sem.at[a, d], recv_sem.at[a, d], {"uly": peer},
            )
            copy.start()
            mine.append(copy)
        sent.append(mine)
        copy = pltpu.make_async_copy(
            src.at[:, pl.ds(pl.multiple_of(me * feat, feat), feat)], here, own_sem.at[a]
        )
        copy.start()
        kept.append(copy)
    halos = []
    for a, out in enumerate((k_out, v_out)):
        kept[a].wait()
        for copy in sent[a]:
            copy.wait_recv()
        for i, (src, dst, side) in enumerate(((rows, 0, right), (halo, halo + rows, left))):
            copy = remote(
                out.at[pl.ds(src, halo)], out.at[pl.ds(dst, halo)],
                halo_send.at[a, i], halo_recv.at[a, i], {"blk": side},
            )
            copy.start()
            halos.append(copy)
    for a in (2, 3):
        kept[a].wait()
        for copy in sent[a]:
            copy.wait_recv()
    for mine in sent:
        for copy in mine:
            copy.wait_send()
    for copy in halos:
        copy.wait()


def spread(n, q, k, v, do):
    part, width = q.shape
    rows, feat = part * n, width // n
    halo = REACHB * BS
    hbm = pl.BlockSpec(memory_space=pl.ANY)
    flat = jax.ShapeDtypeStruct((rows, feat), q.dtype)
    near = jax.ShapeDtypeStruct((rows + 2 * halo, feat), q.dtype)
    return pl.pallas_call(
        functools.partial(spread_kernel, n),
        in_specs=[hbm] * 4,
        out_specs=[hbm] * 4,
        out_shape=[flat, flat, near, near],
        scratch_shapes=[
            pltpu.SemaphoreType.DMA((4, n)),
            pltpu.SemaphoreType.DMA((4, n)),
            pltpu.SemaphoreType.DMA((4,)),
            pltpu.SemaphoreType.DMA((2, 2)),
            pltpu.SemaphoreType.DMA((2, 2)),
        ],
        compiler_params=pltpu.CompilerParams(collective_id=0, has_side_effects=True),
        name="spread",
    )(q, k, v, do)


def collect_kernel(
    n, dq_ref, own_ref, left_ref, right_ref, dq_out, dk_out, dv_out,
    own_scr, res_scr, from_left, from_right,
    send_sem, recv_sem, own_sem, load_sem, halo_send, halo_recv,
):
    me, left, right = greet(n)
    _, rows, feat = own_ref.shape
    halo = left_ref.shape[1]
    part = rows // n
    loads, halos = [], []
    for a in range(2):
        pair = (
            remote(
                left_ref.at[a], from_right.at[a],
                halo_send.at[a, 0], halo_recv.at[a, 0], {"blk": left},
            ),
            remote(
                right_ref.at[a], from_left.at[a],
                halo_send.at[a, 1], halo_recv.at[a, 1], {"blk": right},
            ),
        )
        for copy in pair:
            copy.start()
        halos.append(pair)
        load = pltpu.make_async_copy(own_ref.at[a], own_scr.at[a], load_sem.at[a])
        load.start()
        loads.append(load)
    pending, kept = [], []

    def send(a, src, out):
        there = out.at[:, pl.ds(pl.multiple_of(me * feat, feat), feat)]
        for d in distances(n):
            peer = lax.rem(me + d, n)
            copy = remote(
                src.at[pl.ds(pl.multiple_of(peer * part, part), part)], there,
                send_sem.at[a, d], recv_sem.at[a, d], {"uly": peer},
            )
            copy.start()
            pending.append(copy)
        copy = pltpu.make_async_copy(
            src.at[pl.ds(pl.multiple_of(me * part, part), part)], there, own_sem.at[a]
        )
        copy.start()
        kept.append(copy)

    send(2, dq_ref, dq_out)
    for a in range(2):
        loads[a].wait()

        @pl.loop(halo // BS, (rows - halo) // BS)
        def _(t):
            at = pl.ds(pl.multiple_of(t * BS, BS), BS)
            res_scr[a, at, :] = own_scr[a, at, :].astype(jnp.bfloat16)

    for a, out in enumerate((dk_out, dv_out)):
        for copy in halos[a]:
            copy.wait_recv()

        @pl.loop(0, halo // BS)
        def _(t):
            for base, arrived in ((0, from_left), (rows - halo, from_right)):
                at = pl.ds(pl.multiple_of(base + t * BS, BS), BS)
                more = arrived[a, pl.ds(pl.multiple_of(t * BS, BS), BS), :].astype(jnp.float32)
                res_scr[a, at, :] = (own_scr[a, at, :] + more).astype(jnp.bfloat16)

        send(a, res_scr.at[a], out)
    for copy in kept:
        copy.wait()
    for copy in pending:
        copy.wait()
    for pair in halos:
        for copy in pair:
            copy.wait_send()


def collect(n, dq, own, left, right):
    rows, feat = dq.shape
    halo = left.shape[1]
    bf16 = jnp.bfloat16
    hbm = pl.BlockSpec(memory_space=pl.ANY)
    return pl.pallas_call(
        functools.partial(collect_kernel, n),
        in_specs=[hbm] * 4,
        out_specs=[hbm] * 3,
        out_shape=[jax.ShapeDtypeStruct((rows // n, feat * n), bf16)] * 3,
        scratch_shapes=[
            pltpu.VMEM((2, rows, feat), jnp.float32),
            pltpu.VMEM((2, rows, feat), bf16),
            pltpu.VMEM((2, halo, feat), bf16),
            pltpu.VMEM((2, halo, feat), bf16),
            pltpu.SemaphoreType.DMA((3, n)),
            pltpu.SemaphoreType.DMA((3, n)),
            pltpu.SemaphoreType.DMA((3,)),
            pltpu.SemaphoreType.DMA((2,)),
            pltpu.SemaphoreType.DMA((2, 2)),
            pltpu.SemaphoreType.DMA((2, 2)),
        ],
        compiler_params=pltpu.CompilerParams(
            collective_id=1, has_side_effects=True, vmem_limit_bytes=24 * MIB
        ),
        name="collect",
    )(dq, own, left, right)


def local_lists(key_lists, list_length, per_rank):
    block_rank = lax.axis_index("blk")
    all_blocks = per_rank * lax.axis_size("blk")
    base_block = block_rank * per_rank - REACHB
    lists_here = lax.dynamic_slice_in_dim(key_lists, block_rank * per_rank, per_rank, 0)
    lengths_here = lax.dynamic_slice_in_dim(list_length, block_rank * per_rank, per_rank, 0)
    return (lists_here - base_block) % all_blocks, lengths_here


def shards(queries, keys, values, grad_out, key_lists, list_length):
    n = lax.axis_size("uly")
    q, do, k, v = spread(n, queries, keys, values, grad_out)
    spots, lengths = local_lists(key_lists, list_length, q.shape[0] // BS)
    dq, own, left, right = attend(spots, lengths, q, do, k, v)
    return tuple(collect(n, dq, own, left, right))


def solution(mesh):
    rows = P(("grp", "blk", "uly"), None)
    return jax.shard_map(
        shards,
        mesh=mesh,
        in_specs=(rows, rows, rows, rows, P("grp", None), P("grp")),
        out_specs=(rows, rows, rows),
        check_vma=False,
    )
```

```python
import functools

import jax
import jax.numpy as jnp
from jax import lax
from jax.experimental import pallas as pl
from jax.experimental.pallas import tpu as pltpu
from jax.sharding import PartitionSpec as P

HD = 64
BS = 128
REACHB = 6
PAIR = 2 * HD
SCALE = HD ** (-0.5)
MIB = 1024 * 1024
MESH = pl.DeviceIdType.MESH


def block_diagonal(pair, factor):
    wide = pair.astype(jnp.float32) * factor
    lane = lax.broadcasted_iota(jnp.int32, wide.shape, 1)
    first = jnp.where(lane < HD, wide, 0.0).astype(jnp.bfloat16)
    second = jnp.where(lane < HD, 0.0, wide).astype(jnp.bfloat16)
    return first, second


def attend_kernel(
    spots_ref, lengths_ref, q_ref, do_ref, k_ref, v_ref,
    dq_ref, own_ref, left_ref, right_ref,
    k_scr, v_scr, kt_scr, acc_k, acc_v, s_scr, p_scr, g_scr, w_scr, q_bd, do_bd, q_bdt, do_bdt, dqt_scr, round_scr, sems,
):
    step = pl.program_id(0)
    steps = pl.num_programs(0)
    halo = left_ref.shape[1]
    total, feat = k_scr.shape
    rows = total - 2 * halo
    packs = feat // PAIR

    @pl.when(step == 0)
    def _():
        copies = [
            pltpu.make_async_copy(k_ref, k_scr, sems.at[0]),
            pltpu.make_async_copy(v_ref, v_scr, sems.at[1]),
        ]
        for copy in copies:
            copy.start()

        @pl.loop(0, total // BS)
        def _(b):
            at = pl.ds(b * BS, BS)
            acc_k[at, :] = jnp.zeros((BS, feat), jnp.float32)
            acc_v[at, :] = jnp.zeros((BS, feat), jnp.float32)

        for copy in copies:
            copy.wait()

        @pl.loop(0, total // BS)
        def _(b):
            kt_scr[pl.ds(b * feat, feat), :] = k_scr[pl.ds(b * BS, BS), :].T

    for g in range(packs):
        cols = slice(g * PAIR, (g + 1) * PAIR)
        first, second = block_diagonal(q_ref[:, cols], SCALE)
        q_bd[g, :BS, :] = first
        q_bd[g, BS:, :] = second
        first, second = block_diagonal(do_ref[:, cols], 1.0)
        do_bd[g, :BS, :] = first
        do_bd[g, BS:, :] = second
        q_bdt[g] = q_bd[g].T
        do_bdt[g] = do_bd[g].T

    length = lengths_ref[step]

    def block_of(slot):
        return spots_ref[step, jnp.minimum(slot, length - 1)]

    def products(slot):
        at = pl.ds(pl.multiple_of(block_of(slot) * BS, BS), BS)
        for g in range(packs):
            cols = slice(g * PAIR, (g + 1) * PAIR)
            s_scr[slot, g] = jnp.dot(k_scr[at, cols], q_bdt[g], preferred_element_type=jnp.float32)
            p_scr[slot, g] = jnp.dot(v_scr[at, cols], do_bdt[g], preferred_element_type=jnp.float32)

    def scores(slot, carry):
        out = []
        for g in range(packs):
            top, sums, cross = carry[g]
            s = s_scr[slot, g].reshape(BS // 8, 8, 2 * BS)
            dp = p_scr[slot, g].reshape(BS // 8, 8, 2 * BS)
            new_top = jnp.maximum(top, jnp.max(s, axis=0))
            keep = jnp.exp(top - new_top)
            p = jnp.exp(s - new_top[None])
            out.append(
                (
                    new_top,
                    sums * keep + jnp.sum(p, axis=0),
                    cross * keep + jnp.sum(p * dp, axis=0),
                )
            )
        products(slot + 1)
        return tuple(out)

    products(0)
    blank = jnp.zeros((8, 2 * BS), jnp.float32)
    start = tuple((blank - jnp.inf, blank, blank) for _ in range(packs))
    stats = lax.fori_loop(0, length, scores, start)
    merged = []
    for top, sums, cross in stats:
        best = jnp.max(top, axis=0, keepdims=True)
        factor = jnp.exp(top - best)
        denom = jnp.sum(sums * factor, axis=0, keepdims=True)
        delta = jnp.sum(cross * factor, axis=0, keepdims=True) / denom
        merged.append((best + jnp.log(denom), delta))

    dqt_scr[...] = jnp.zeros_like(dqt_scr)

    def weights(slot):
        for g in range(packs):
            log_total, delta = merged[g]
            weight = jnp.exp(s_scr[slot, g] - log_total)
            g_scr[slot, g] = (weight * (p_scr[slot, g] - delta)).astype(jnp.bfloat16)
            w_scr[slot, g] = weight.astype(jnp.bfloat16)

    def sums(slot):
        spot = block_of(slot)
        at = pl.ds(pl.multiple_of(spot * BS, BS), BS)
        for g in range(packs):
            cols = slice(g * PAIR, (g + 1) * PAIR)
            grad = g_scr[slot, g]
            acc_v[at, cols] += jnp.dot(w_scr[slot, g], do_bd[g], preferred_element_type=jnp.float32)
            acc_k[at, cols] += jnp.dot(grad, q_bd[g], preferred_element_type=jnp.float32)
            for h in range(2):
                low = g * PAIR + h * HD
                kt = kt_scr[pl.ds(pl.multiple_of(spot * feat + low, HD), HD), :]
                dqt_scr[low : low + HD, :] += jnp.dot(
                    kt, grad[:, h * BS : (h + 1) * BS], preferred_element_type=jnp.float32
                )

    weights(0)

    @pl.loop(1, length)
    def _(slot):
        sums(slot - 1)
        weights(slot)

    sums(length - 1)

    dq_ref[...] = (dqt_scr[...].T * SCALE).astype(jnp.bfloat16)

    @pl.when(step == steps - 1)
    def _():
        for i, acc in enumerate((acc_k, acc_v)):
            for side, base in enumerate((0, halo + rows)):

                @pl.loop(0, halo // BS)
                def _(b):
                    round_scr[i, side, pl.ds(b * BS, BS), :] = acc[
                        pl.ds(base + b * BS, BS), :
                    ].astype(jnp.bfloat16)

        copies = []
        for i, acc in enumerate((acc_k, acc_v)):
            copies += [
                pltpu.make_async_copy(acc.at[pl.ds(halo, rows)], own_ref.at[i], sems.at[3 * i]),
                pltpu.make_async_copy(round_scr.at[i, 0], left_ref.at[i], sems.at[3 * i + 1]),
                pltpu.make_async_copy(round_scr.at[i, 1], right_ref.at[i], sems.at[3 * i + 2]),
            ]
        for copy in copies:
            copy.start()
        for copy in copies:
            copy.wait()


def attend(spots, lengths, q, do, k, v):
    rows, feat = q.shape
    total = k.shape[0]
    halo = (total - rows) // 2
    packs = feat // PAIR
    slots = spots.shape[1]
    hbm = pl.BlockSpec(memory_space=pl.ANY)
    block = pl.BlockSpec((BS, feat), lambda i, *_: (i, 0))
    f32, bf16 = jnp.float32, jnp.bfloat16
    return pl.pallas_call(
        attend_kernel,
        grid_spec=pltpu.PrefetchScalarGridSpec(
            num_scalar_prefetch=2,
            grid=(rows // BS,),
            in_specs=[block, block] + [hbm] * 2,
            out_specs=[block, hbm, hbm, hbm],
            scratch_shapes=[
                pltpu.VMEM((total, feat), bf16),
                pltpu.VMEM((total, feat), bf16),
                pltpu.VMEM((total // BS * feat, BS), bf16),
                pltpu.VMEM((total, feat), f32),
                pltpu.VMEM((total, feat), f32),
                pltpu.VMEM((slots + 1, packs, BS, 2 * BS), f32),
                pltpu.VMEM((slots + 1, packs, BS, 2 * BS), f32),
                pltpu.VMEM((slots, packs, BS, 2 * BS), bf16),
                pltpu.VMEM((slots, packs, BS, 2 * BS), bf16),
                pltpu.VMEM((packs, 2 * BS, PAIR), bf16),
                pltpu.VMEM((packs, 2 * BS, PAIR), bf16),
                pltpu.VMEM((packs, PAIR, 2 * BS), bf16),
                pltpu.VMEM((packs, PAIR, 2 * BS), bf16),
                pltpu.VMEM((feat, BS), f32),
                pltpu.VMEM((2, 2, halo, feat), bf16),
                pltpu.SemaphoreType.DMA((6,)),
            ],
        ),
        out_shape=[
            jax.ShapeDtypeStruct((rows, feat), bf16),
            jax.ShapeDtypeStruct((2, rows, feat), f32),
            jax.ShapeDtypeStruct((2, halo, feat), bf16),
            jax.ShapeDtypeStruct((2, halo, feat), bf16),
        ],
        compiler_params=pltpu.CompilerParams(vmem_limit_bytes=60 * MIB),
        name="attend",
    )(spots, lengths, q, do, k, v)


def greet(n):
    me = lax.axis_index("uly")
    count = lax.axis_size("blk")
    rank = lax.axis_index("blk")
    left, right = lax.rem(rank + count - 1, count), lax.rem(rank + 1, count)
    barrier = pltpu.get_barrier_semaphore()
    for d in range(1, n):
        pl.semaphore_signal(barrier, 1, device_id={"uly": lax.rem(me + d, n)}, device_id_type=MESH)
    for side in (left, right):
        pl.semaphore_signal(barrier, 1, device_id={"blk": side}, device_id_type=MESH)
    pl.semaphore_wait(barrier, n + 1)
    return me, left, right


def remote(src, dst, send, recv, where):
    return pltpu.make_async_remote_copy(
        src_ref=src, dst_ref=dst, send_sem=send, recv_sem=recv, device_id=where, device_id_type=MESH
    )


def distances(n):
    return sorted(range(1, n), key=lambda d: -min(d, n - d))


def spread_kernel(
    n, q_ref, k_ref, v_ref, do_ref, q_out, do_out, k_out, v_out,
    send_sem, recv_sem, own_sem, halo_send, halo_recv,
):
    me, left, right = greet(n)
    part = q_ref.shape[0]
    rows, feat = q_out.shape
    halo = (k_out.shape[0] - rows) // 2
    arrays = ((k_ref, k_out, halo), (v_ref, v_out, halo), (q_ref, q_out, 0), (do_ref, do_out, 0))
    sent, kept = [], []
    for a, (src, dst, offset) in enumerate(arrays):
        here = dst.at[pl.ds(pl.multiple_of(offset + me * part, BS), part)]
        mine = []
        for d in distances(n):
            peer = lax.rem(me + d, n)
            copy = remote(
                src.at[:, pl.ds(pl.multiple_of(peer * feat, feat), feat)], here,
                send_sem.at[a, d], recv_sem.at[a, d], {"uly": peer},
            )
            copy.start()
            mine.append(copy)
        sent.append(mine)
        copy = pltpu.make_async_copy(
            src.at[:, pl.ds(pl.multiple_of(me * feat, feat), feat)], here, own_sem.at[a]
        )
        copy.start()
        kept.append(copy)
    halos = []
    for a, out in enumerate((k_out, v_out)):
        kept[a].wait()
        for copy in sent[a]:
            copy.wait_recv()
        for i, (src, dst, side) in enumerate(((rows, 0, right), (halo, halo + rows, left))):
            copy = remote(
                out.at[pl.ds(src, halo)], out.at[pl.ds(dst, halo)],
                halo_send.at[a, i], halo_recv.at[a, i], {"blk": side},
            )
            copy.start()
            halos.append(copy)
    for a in (2, 3):
        kept[a].wait()
        for copy in sent[a]:
            copy.wait_recv()
    for mine in sent:
        for copy in mine:
            copy.wait_send()
    for copy in halos:
        copy.wait()


def spread(n, q, k, v, do):
    part, width = q.shape
    rows, feat = part * n, width // n
    halo = REACHB * BS
    hbm = pl.BlockSpec(memory_space=pl.ANY)
    flat = jax.ShapeDtypeStruct((rows, feat), q.dtype)
    near = jax.ShapeDtypeStruct((rows + 2 * halo, feat), q.dtype)
    return pl.pallas_call(
        functools.partial(spread_kernel, n),
        in_specs=[hbm] * 4,
        out_specs=[hbm] * 4,
        out_shape=[flat, flat, near, near],
        scratch_shapes=[
            pltpu.SemaphoreType.DMA((4, n)),
            pltpu.SemaphoreType.DMA((4, n)),
            pltpu.SemaphoreType.DMA((4,)),
            pltpu.SemaphoreType.DMA((2, 2)),
            pltpu.SemaphoreType.DMA((2, 2)),
        ],
        compiler_params=pltpu.CompilerParams(collective_id=0, has_side_effects=True),
        name="spread",
    )(q, k, v, do)


def collect_kernel(
    n, dq_ref, own_ref, left_ref, right_ref, dq_out, dk_out, dv_out,
    own_scr, res_scr, from_left, from_right,
    send_sem, recv_sem, own_sem, load_sem, halo_send, halo_recv,
):
    me, left, right = greet(n)
    _, rows, feat = own_ref.shape
    halo = left_ref.shape[1]
    part = rows // n
    loads, halos = [], []
    for a in range(2):
        pair = (
            remote(
                left_ref.at[a], from_right.at[a],
                halo_send.at[a, 0], halo_recv.at[a, 0], {"blk": left},
            ),
            remote(
                right_ref.at[a], from_left.at[a],
                halo_send.at[a, 1], halo_recv.at[a, 1], {"blk": right},
            ),
        )
        for copy in pair:
            copy.start()
        halos.append(pair)
        load = pltpu.make_async_copy(own_ref.at[a], own_scr.at[a], load_sem.at[a])
        load.start()
        loads.append(load)
    pending, kept = [], []

    def send(a, src, out):
        there = out.at[:, pl.ds(pl.multiple_of(me * feat, feat), feat)]
        for d in distances(n):
            peer = lax.rem(me + d, n)
            copy = remote(
                src.at[pl.ds(pl.multiple_of(peer * part, part), part)], there,
                send_sem.at[a, d], recv_sem.at[a, d], {"uly": peer},
            )
            copy.start()
            pending.append(copy)
        copy = pltpu.make_async_copy(
            src.at[pl.ds(pl.multiple_of(me * part, part), part)], there, own_sem.at[a]
        )
        copy.start()
        kept.append(copy)

    send(2, dq_ref, dq_out)
    for a in range(2):
        loads[a].wait()

        @pl.loop(halo // BS, (rows - halo) // BS)
        def _(t):
            at = pl.ds(pl.multiple_of(t * BS, BS), BS)
            res_scr[a, at, :] = own_scr[a, at, :].astype(jnp.bfloat16)

    for a, out in enumerate((dk_out, dv_out)):
        for copy in halos[a]:
            copy.wait_recv()

        @pl.loop(0, halo // BS)
        def _(t):
            for base, arrived in ((0, from_left), (rows - halo, from_right)):
                at = pl.ds(pl.multiple_of(base + t * BS, BS), BS)
                more = arrived[a, pl.ds(pl.multiple_of(t * BS, BS), BS), :].astype(jnp.float32)
                res_scr[a, at, :] = (own_scr[a, at, :] + more).astype(jnp.bfloat16)

        send(a, res_scr.at[a], out)
    for copy in kept:
        copy.wait()
    for copy in pending:
        copy.wait()
    for pair in halos:
        for copy in pair:
            copy.wait_send()


def collect(n, dq, own, left, right):
    rows, feat = dq.shape
    halo = left.shape[1]
    bf16 = jnp.bfloat16
    hbm = pl.BlockSpec(memory_space=pl.ANY)
    return pl.pallas_call(
        functools.partial(collect_kernel, n),
        in_specs=[hbm] * 4,
        out_specs=[hbm] * 3,
        out_shape=[jax.ShapeDtypeStruct((rows // n, feat * n), bf16)] * 3,
        scratch_shapes=[
            pltpu.VMEM((2, rows, feat), jnp.float32),
            pltpu.VMEM((2, rows, feat), bf16),
            pltpu.VMEM((2, halo, feat), bf16),
            pltpu.VMEM((2, halo, feat), bf16),
            pltpu.SemaphoreType.DMA((3, n)),
            pltpu.SemaphoreType.DMA((3, n)),
            pltpu.SemaphoreType.DMA((3,)),
            pltpu.SemaphoreType.DMA((2,)),
            pltpu.SemaphoreType.DMA((2, 2)),
            pltpu.SemaphoreType.DMA((2, 2)),
        ],
        compiler_params=pltpu.CompilerParams(
            collective_id=1, has_side_effects=True, vmem_limit_bytes=60 * MIB
        ),
        name="collect",
    )(dq, own, left, right)


def local_lists(key_lists, list_length, per_rank):
    block_rank = lax.axis_index("blk")
    all_blocks = per_rank * lax.axis_size("blk")
    base_block = block_rank * per_rank - REACHB
    lists_here = lax.dynamic_slice_in_dim(key_lists, block_rank * per_rank, per_rank, 0)
    lengths_here = lax.dynamic_slice_in_dim(list_length, block_rank * per_rank, per_rank, 0)
    return (lists_here - base_block) % all_blocks, lengths_here


def shards(queries, keys, values, grad_out, key_lists, list_length):
    n = lax.axis_size("uly")
    q, do, k, v = spread(n, queries, keys, values, grad_out)
    spots, lengths = local_lists(key_lists, list_length, q.shape[0] // BS)
    dq, own, left, right = attend(spots, lengths, q, do, k, v)
    return tuple(collect(n, dq, own, left, right))


def solution(mesh):
    rows = P(("grp", "blk", "uly"), None)
    return jax.shard_map(
        shards,
        mesh=mesh,
        in_specs=(rows, rows, rows, rows, P("grp", None), P("grp")),
        out_specs=(rows, rows, rows),
        check_vma=False,
    )
```

```python
import functools

import jax
import jax.numpy as jnp
from jax import lax
from jax.experimental import pallas as pl
from jax.experimental.pallas import tpu as pltpu
from jax.sharding import PartitionSpec as P

HD = 64
BS = 128
REACHB = 6
PAIR = 2 * HD
SCALE = HD ** (-0.5)
GROUPS = (4, 2, 1)
MIB = 1024 * 1024
MESH = pl.DeviceIdType.MESH


def block_diagonal(pair, factor):
    wide = pair.astype(jnp.float32) * factor
    lane = lax.broadcasted_iota(jnp.int32, wide.shape, 1)
    first = jnp.where(lane < HD, wide, 0.0).astype(jnp.bfloat16)
    second = jnp.where(lane < HD, 0.0, wide).astype(jnp.bfloat16)
    return first, second


def attend_kernel(
    spots_ref, lengths_ref, q_ref, do_ref, k_ref, v_ref,
    dq_ref, own_ref, left_ref, right_ref,
    k_scr, v_scr, kt_scr, acc_k, acc_v, s_scr, p_scr, q_bd, do_bd, q_bdt, do_bdt, dqt_scr, round_scr, sems,
):
    step = pl.program_id(0)
    steps = pl.num_programs(0)
    halo = left_ref.shape[1]
    total, feat = k_scr.shape
    rows = total - 2 * halo
    packs = feat // PAIR

    @pl.when(step == 0)
    def _():
        copies = [
            pltpu.make_async_copy(k_ref, k_scr, sems.at[0]),
            pltpu.make_async_copy(v_ref, v_scr, sems.at[1]),
        ]
        for copy in copies:
            copy.start()

        @pl.loop(0, total // BS)
        def _(b):
            at = pl.ds(b * BS, BS)
            acc_k[at, :] = jnp.zeros((BS, feat), jnp.float32)
            acc_v[at, :] = jnp.zeros((BS, feat), jnp.float32)

        for copy in copies:
            copy.wait()

        @pl.loop(0, total // BS, unroll=4)
        def _(b):
            kt_scr[pl.ds(b * feat, feat), :] = k_scr[pl.ds(b * BS, BS), :].T

    for g in range(packs):
        cols = slice(g * PAIR, (g + 1) * PAIR)
        first, second = block_diagonal(q_ref[:, cols], SCALE)
        q_bd[g, :BS, :] = first
        q_bd[g, BS:, :] = second
        first, second = block_diagonal(do_ref[:, cols], 1.0)
        do_bd[g, :BS, :] = first
        do_bd[g, BS:, :] = second
        q_bdt[g] = q_bd[g].T
        do_bdt[g] = do_bd[g].T

    length = lengths_ref[step]
    groups, done = [], 0
    for taken in GROUPS:
        count = (length - done) // taken
        groups.append((taken, done, count))
        done = done + taken * count

    def rows_of(slot, taken):
        spots = [spots_ref[step, slot + i] for i in range(taken)]
        return spots, [pl.ds(pl.multiple_of(spot * BS, BS), BS) for spot in spots]

    def joined(pieces, axis=0):
        return pieces[0] if len(pieces) == 1 else jnp.concatenate(pieces, axis=axis)

    def scores(slot, carry, taken):
        _, ats = rows_of(slot, taken)
        out = []
        for g in range(packs):
            top, sums, cross = carry[g]
            cols = slice(g * PAIR, (g + 1) * PAIR)
            keys = joined([k_scr[at, cols] for at in ats])
            values = joined([v_scr[at, cols] for at in ats])
            s = jnp.dot(keys, q_bdt[g], preferred_element_type=jnp.float32)
            dp = jnp.dot(values, do_bdt[g], preferred_element_type=jnp.float32)
            for i in range(taken):
                s_scr[slot + i, g] = s[i * BS : (i + 1) * BS]
                p_scr[slot + i, g] = dp[i * BS : (i + 1) * BS]
            s = s.reshape(taken * BS // 8, 8, 2 * BS)
            dp = dp.reshape(taken * BS // 8, 8, 2 * BS)
            new_top = jnp.maximum(top, jnp.max(s, axis=0))
            keep = jnp.exp(top - new_top)
            p = jnp.exp(s - new_top[None])
            out.append(
                (
                    new_top,
                    sums * keep + jnp.sum(p, axis=0),
                    cross * keep + jnp.sum(p * dp, axis=0),
                )
            )
        return tuple(out)

    blank = jnp.zeros((8, 2 * BS), jnp.float32)
    start = tuple((blank - jnp.inf, blank, blank) for _ in range(packs))
    stats = start
    for taken, first, count in groups:
        stats = lax.fori_loop(
            0,
            count,
            lambda j, c, taken=taken, first=first: scores(first + taken * j, c, taken),
            stats,
        )
    merged = []
    for top, sums, cross in stats:
        best = jnp.max(top, axis=0, keepdims=True)
        factor = jnp.exp(top - best)
        denom = jnp.sum(sums * factor, axis=0, keepdims=True)
        delta = jnp.sum(cross * factor, axis=0, keepdims=True) / denom
        merged.append((best + jnp.log(denom), delta))

    dqt_scr[...] = jnp.zeros_like(dqt_scr)

    def gradients(slot, taken):
        spots, ats = rows_of(slot, taken)
        for g in range(packs):
            log_total, delta = merged[g]
            cols = slice(g * PAIR, (g + 1) * PAIR)
            halves, grads = [], []
            for i in range(taken):
                weight = jnp.exp(s_scr[slot + i, g] - log_total)
                grads.append((weight * (p_scr[slot + i, g] - delta)).astype(jnp.bfloat16))
                halves.append(weight.astype(jnp.bfloat16))
            grad, half = joined(grads), joined(halves)
            dv = jnp.dot(half, do_bd[g], preferred_element_type=jnp.float32)
            dk = jnp.dot(grad, q_bd[g], preferred_element_type=jnp.float32)
            for i, at in enumerate(ats):
                acc_v[at, cols] += dv[i * BS : (i + 1) * BS]
                acc_k[at, cols] += dk[i * BS : (i + 1) * BS]
            for h in range(2):
                low = g * PAIR + h * HD
                kt = joined(
                    [kt_scr[pl.ds(pl.multiple_of(spot * feat + low, HD), HD), :] for spot in spots], 1
                )
                dqt_scr[low : low + HD, :] += jnp.dot(
                    kt, grad[:, h * BS : (h + 1) * BS], preferred_element_type=jnp.float32
                )

    for taken, first, count in groups:

        @pl.loop(0, count)
        def _(j):
            gradients(first + taken * j, taken)

    dq_ref[...] = (dqt_scr[...].T * SCALE).astype(jnp.bfloat16)

    @pl.when(step == steps - 1)
    def _():
        for i, acc in enumerate((acc_k, acc_v)):
            for side, base in enumerate((0, halo + rows)):

                @pl.loop(0, halo // BS)
                def _(b):
                    round_scr[i, side, pl.ds(b * BS, BS), :] = acc[
                        pl.ds(base + b * BS, BS), :
                    ].astype(jnp.bfloat16)

        copies = []
        for i, acc in enumerate((acc_k, acc_v)):
            copies += [
                pltpu.make_async_copy(acc.at[pl.ds(halo, rows)], own_ref.at[i], sems.at[3 * i]),
                pltpu.make_async_copy(round_scr.at[i, 0], left_ref.at[i], sems.at[3 * i + 1]),
                pltpu.make_async_copy(round_scr.at[i, 1], right_ref.at[i], sems.at[3 * i + 2]),
            ]
        for copy in copies:
            copy.start()
        for copy in copies:
            copy.wait()


def attend(spots, lengths, q, do, k, v):
    rows, feat = q.shape
    total = k.shape[0]
    halo = (total - rows) // 2
    packs = feat // PAIR
    slots = spots.shape[1]
    hbm = pl.BlockSpec(memory_space=pl.ANY)
    block = pl.BlockSpec((BS, feat), lambda i, *_: (i, 0))
    f32, bf16 = jnp.float32, jnp.bfloat16
    return pl.pallas_call(
        attend_kernel,
        grid_spec=pltpu.PrefetchScalarGridSpec(
            num_scalar_prefetch=2,
            grid=(rows // BS,),
            in_specs=[block, block] + [hbm] * 2,
            out_specs=[block, hbm, hbm, hbm],
            scratch_shapes=[
                pltpu.VMEM((total, feat), bf16),
                pltpu.VMEM((total, feat), bf16),
                pltpu.VMEM((total // BS * feat, BS), bf16),
                pltpu.VMEM((total, feat), f32),
                pltpu.VMEM((total, feat), f32),
                pltpu.VMEM((slots, packs, BS, 2 * BS), f32),
                pltpu.VMEM((slots, packs, BS, 2 * BS), f32),
                pltpu.VMEM((packs, 2 * BS, PAIR), bf16),
                pltpu.VMEM((packs, 2 * BS, PAIR), bf16),
                pltpu.VMEM((packs, PAIR, 2 * BS), bf16),
                pltpu.VMEM((packs, PAIR, 2 * BS), bf16),
                pltpu.VMEM((feat, BS), f32),
                pltpu.VMEM((2, 2, halo, feat), bf16),
                pltpu.SemaphoreType.DMA((6,)),
            ],
        ),
        out_shape=[
            jax.ShapeDtypeStruct((rows, feat), bf16),
            jax.ShapeDtypeStruct((2, rows, feat), f32),
            jax.ShapeDtypeStruct((2, halo, feat), bf16),
            jax.ShapeDtypeStruct((2, halo, feat), bf16),
        ],
        compiler_params=pltpu.CompilerParams(vmem_limit_bytes=60 * MIB),
        name="attend",
    )(spots, lengths, q, do, k, v)


def greet(n):
    me = lax.axis_index("uly")
    count = lax.axis_size("blk")
    rank = lax.axis_index("blk")
    left, right = lax.rem(rank + count - 1, count), lax.rem(rank + 1, count)
    barrier = pltpu.get_barrier_semaphore()
    for d in range(1, n):
        pl.semaphore_signal(barrier, 1, device_id={"uly": lax.rem(me + d, n)}, device_id_type=MESH)
    for side in (left, right):
        pl.semaphore_signal(barrier, 1, device_id={"blk": side}, device_id_type=MESH)
    pl.semaphore_wait(barrier, n + 1)
    return me, left, right


def remote(src, dst, send, recv, where):
    return pltpu.make_async_remote_copy(
        src_ref=src, dst_ref=dst, send_sem=send, recv_sem=recv, device_id=where, device_id_type=MESH
    )


def distances(n):
    return sorted(range(1, n), key=lambda d: -min(d, n - d))


def spread_kernel(
    n, q_ref, k_ref, v_ref, do_ref, q_out, do_out, k_out, v_out,
    send_sem, recv_sem, own_sem, halo_send, halo_recv,
):
    me, left, right = greet(n)
    part = q_ref.shape[0]
    rows, feat = q_out.shape
    halo = (k_out.shape[0] - rows) // 2
    arrays = ((k_ref, k_out, halo), (v_ref, v_out, halo), (q_ref, q_out, 0), (do_ref, do_out, 0))
    sent, kept = [], []
    for a, (src, dst, offset) in enumerate(arrays):
        here = dst.at[pl.ds(pl.multiple_of(offset + me * part, BS), part)]
        mine = []
        for d in distances(n):
            peer = lax.rem(me + d, n)
            copy = remote(
                src.at[:, pl.ds(pl.multiple_of(peer * feat, feat), feat)], here,
                send_sem.at[a, d], recv_sem.at[a, d], {"uly": peer},
            )
            copy.start()
            mine.append(copy)
        sent.append(mine)
        copy = pltpu.make_async_copy(
            src.at[:, pl.ds(pl.multiple_of(me * feat, feat), feat)], here, own_sem.at[a]
        )
        copy.start()
        kept.append(copy)
    halos = []
    for a, out in enumerate((k_out, v_out)):
        kept[a].wait()
        for copy in sent[a]:
            copy.wait_recv()
        for i, (src, dst, side) in enumerate(((rows, 0, right), (halo, halo + rows, left))):
            copy = remote(
                out.at[pl.ds(src, halo)], out.at[pl.ds(dst, halo)],
                halo_send.at[a, i], halo_recv.at[a, i], {"blk": side},
            )
            copy.start()
            halos.append(copy)
    for a in (2, 3):
        kept[a].wait()
        for copy in sent[a]:
            copy.wait_recv()
    for mine in sent:
        for copy in mine:
            copy.wait_send()
    for copy in halos:
        copy.wait()


def spread(n, q, k, v, do):
    part, width = q.shape
    rows, feat = part * n, width // n
    halo = REACHB * BS
    hbm = pl.BlockSpec(memory_space=pl.ANY)
    flat = jax.ShapeDtypeStruct((rows, feat), q.dtype)
    near = jax.ShapeDtypeStruct((rows + 2 * halo, feat), q.dtype)
    return pl.pallas_call(
        functools.partial(spread_kernel, n),
        in_specs=[hbm] * 4,
        out_specs=[hbm] * 4,
        out_shape=[flat, flat, near, near],
        scratch_shapes=[
            pltpu.SemaphoreType.DMA((4, n)),
            pltpu.SemaphoreType.DMA((4, n)),
            pltpu.SemaphoreType.DMA((4,)),
            pltpu.SemaphoreType.DMA((2, 2)),
            pltpu.SemaphoreType.DMA((2, 2)),
        ],
        compiler_params=pltpu.CompilerParams(collective_id=0, has_side_effects=True),
        name="spread",
    )(q, k, v, do)


def collect_kernel(
    n, dq_ref, own_ref, left_ref, right_ref, dq_out, dk_out, dv_out,
    own_scr, res_scr, from_left, from_right,
    send_sem, recv_sem, own_sem, load_sem, halo_send, halo_recv,
):
    me, left, right = greet(n)
    _, rows, feat = own_ref.shape
    halo = left_ref.shape[1]
    part = rows // n
    loads, halos = [], []
    for a in range(2):
        pair = (
            remote(
                left_ref.at[a], from_right.at[a],
                halo_send.at[a, 0], halo_recv.at[a, 0], {"blk": left},
            ),
            remote(
                right_ref.at[a], from_left.at[a],
                halo_send.at[a, 1], halo_recv.at[a, 1], {"blk": right},
            ),
        )
        for copy in pair:
            copy.start()
        halos.append(pair)
        load = pltpu.make_async_copy(own_ref.at[a], own_scr.at[a], load_sem.at[a])
        load.start()
        loads.append(load)
    pending, kept = [], []

    def send(a, src, out):
        there = out.at[:, pl.ds(pl.multiple_of(me * feat, feat), feat)]
        for d in distances(n):
            peer = lax.rem(me + d, n)
            copy = remote(
                src.at[pl.ds(pl.multiple_of(peer * part, part), part)], there,
                send_sem.at[a, d], recv_sem.at[a, d], {"uly": peer},
            )
            copy.start()
            pending.append(copy)
        copy = pltpu.make_async_copy(
            src.at[pl.ds(pl.multiple_of(me * part, part), part)], there, own_sem.at[a]
        )
        copy.start()
        kept.append(copy)

    send(2, dq_ref, dq_out)
    for a in range(2):
        loads[a].wait()

        @pl.loop(halo // BS, (rows - halo) // BS)
        def _(t):
            at = pl.ds(pl.multiple_of(t * BS, BS), BS)
            res_scr[a, at, :] = own_scr[a, at, :].astype(jnp.bfloat16)

    for a, out in enumerate((dk_out, dv_out)):
        for copy in halos[a]:
            copy.wait_recv()

        @pl.loop(0, halo // BS)
        def _(t):
            for base, arrived in ((0, from_left), (rows - halo, from_right)):
                at = pl.ds(pl.multiple_of(base + t * BS, BS), BS)
                more = arrived[a, pl.ds(pl.multiple_of(t * BS, BS), BS), :].astype(jnp.float32)
                res_scr[a, at, :] = (own_scr[a, at, :] + more).astype(jnp.bfloat16)

        send(a, res_scr.at[a], out)
    for copy in kept:
        copy.wait()
    for copy in pending:
        copy.wait()
    for pair in halos:
        for copy in pair:
            copy.wait_send()


def collect(n, dq, own, left, right):
    rows, feat = dq.shape
    halo = left.shape[1]
    bf16 = jnp.bfloat16
    hbm = pl.BlockSpec(memory_space=pl.ANY)
    return pl.pallas_call(
        functools.partial(collect_kernel, n),
        in_specs=[hbm] * 4,
        out_specs=[hbm] * 3,
        out_shape=[jax.ShapeDtypeStruct((rows // n, feat * n), bf16)] * 3,
        scratch_shapes=[
            pltpu.VMEM((2, rows, feat), jnp.float32),
            pltpu.VMEM((2, rows, feat), bf16),
            pltpu.VMEM((2, halo, feat), bf16),
            pltpu.VMEM((2, halo, feat), bf16),
            pltpu.SemaphoreType.DMA((3, n)),
            pltpu.SemaphoreType.DMA((3, n)),
            pltpu.SemaphoreType.DMA((3,)),
            pltpu.SemaphoreType.DMA((2,)),
            pltpu.SemaphoreType.DMA((2, 2)),
            pltpu.SemaphoreType.DMA((2, 2)),
        ],
        compiler_params=pltpu.CompilerParams(
            collective_id=1, has_side_effects=True, vmem_limit_bytes=60 * MIB
        ),
        name="collect",
    )(dq, own, left, right)


def local_lists(key_lists, list_length, per_rank):
    block_rank = lax.axis_index("blk")
    all_blocks = per_rank * lax.axis_size("blk")
    base_block = block_rank * per_rank - REACHB
    lists_here = lax.dynamic_slice_in_dim(key_lists, block_rank * per_rank, per_rank, 0)
    lengths_here = lax.dynamic_slice_in_dim(list_length, block_rank * per_rank, per_rank, 0)
    return (lists_here - base_block) % all_blocks, lengths_here


def shards(queries, keys, values, grad_out, key_lists, list_length):
    n = lax.axis_size("uly")
    q, do, k, v = spread(n, queries, keys, values, grad_out)
    spots, lengths = local_lists(key_lists, list_length, q.shape[0] // BS)
    dq, own, left, right = attend(spots, lengths, q, do, k, v)
    return tuple(collect(n, dq, own, left, right))


def solution(mesh):
    rows = P(("grp", "blk", "uly"), None)
    return jax.shard_map(
        shards,
        mesh=mesh,
        in_specs=(rows, rows, rows, rows, P("grp", None), P("grp")),
        out_specs=(rows, rows, rows),
        check_vma=False,
    )
```

```python
import functools

import jax
import jax.numpy as jnp
from jax import lax
from jax.experimental import pallas as pl
from jax.experimental.pallas import tpu as pltpu
from jax.sharding import PartitionSpec as P

HD = 64
BS = 128
REACHB = 6
PAIR = 2 * HD
SCALE = HD ** (-0.5)
GROUPS = (4, 2, 1)
MIB = 1024 * 1024
MESH = pl.DeviceIdType.MESH


def block_diagonal(pair, factor):
    wide = pair.astype(jnp.float32) * factor
    lane = lax.broadcasted_iota(jnp.int32, wide.shape, 1)
    first = jnp.where(lane < HD, wide, 0.0).astype(jnp.bfloat16)
    second = jnp.where(lane < HD, 0.0, wide).astype(jnp.bfloat16)
    return first, second


def attend_kernel(
    spots_ref, lengths_ref, q_ref, do_ref, k_ref, v_ref,
    dq_ref, own_ref, left_ref, right_ref,
    k_scr, v_scr, kt_scr, acc_k, acc_v, s_scr, p_scr, q_bd, do_bd, q_bdt, do_bdt, dqt_scr, round_scr, sems,
):
    step = pl.program_id(0)
    steps = pl.num_programs(0)
    halo = left_ref.shape[1]
    total, feat = k_scr.shape
    rows = total - 2 * halo
    packs = feat // PAIR

    @pl.when(step == 0)
    def _():
        copies = [
            pltpu.make_async_copy(k_ref, k_scr, sems.at[0]),
            pltpu.make_async_copy(v_ref, v_scr, sems.at[1]),
        ]
        for copy in copies:
            copy.start()

        @pl.loop(0, total // BS)
        def _(b):
            at = pl.ds(b * BS, BS)
            acc_k[at, :] = jnp.zeros((BS, feat), jnp.float32)
            acc_v[at, :] = jnp.zeros((BS, feat), jnp.float32)

        for copy in copies:
            copy.wait()

        @pl.loop(0, total // BS, unroll=4)
        def _(b):
            kt_scr[pl.ds(b * feat, feat), :] = k_scr[pl.ds(b * BS, BS), :].T

    for g in range(packs):
        cols = slice(g * PAIR, (g + 1) * PAIR)
        first, second = block_diagonal(q_ref[:, cols], SCALE)
        q_bd[g, :BS, :] = first
        q_bd[g, BS:, :] = second
        first, second = block_diagonal(do_ref[:, cols], 1.0)
        do_bd[g, :BS, :] = first
        do_bd[g, BS:, :] = second
        q_bdt[g] = q_bd[g].T
        do_bdt[g] = do_bd[g].T

    length = lengths_ref[step]
    groups, done = [], 0
    for taken in GROUPS:
        count = (length - done) // taken
        groups.append((taken, done, count))
        done = done + taken * count

    def rows_of(slot, taken):
        spots = [spots_ref[step, slot + i] for i in range(taken)]
        return spots, [pl.ds(pl.multiple_of(spot * BS, BS), BS) for spot in spots]

    def joined(pieces, axis=0):
        return pieces[0] if len(pieces) == 1 else jnp.concatenate(pieces, axis=axis)

    def scores(slot, carry, taken):
        _, ats = rows_of(slot, taken)
        out = []
        for g in range(packs):
            top, sums, cross = carry[g]
            cols = slice(g * PAIR, (g + 1) * PAIR)
            keys = joined([k_scr[at, cols] for at in ats])
            values = joined([v_scr[at, cols] for at in ats])
            s = jnp.dot(keys, q_bdt[g], preferred_element_type=jnp.float32)
            dp = jnp.dot(values, do_bdt[g], preferred_element_type=jnp.float32)
            for i in range(taken):
                s_scr[slot + i, g] = s[i * BS : (i + 1) * BS]
                p_scr[slot + i, g] = dp[i * BS : (i + 1) * BS]
            s = s.reshape(taken * BS // 8, 8, 2 * BS)
            dp = dp.reshape(taken * BS // 8, 8, 2 * BS)
            new_top = jnp.maximum(top, jnp.max(s, axis=0))
            keep = jnp.exp(top - new_top)
            p = jnp.exp(s - new_top[None])
            out.append(
                (
                    new_top,
                    sums * keep + jnp.sum(p, axis=0),
                    cross * keep + jnp.sum(p * dp, axis=0),
                )
            )
        return tuple(out)

    blank = jnp.zeros((8, 2 * BS), jnp.float32)
    start = tuple((blank - jnp.inf, blank, blank) for _ in range(packs))
    stats = start
    for taken, first, count in groups:
        stats = lax.fori_loop(
            0,
            count,
            lambda j, c, taken=taken, first=first: scores(first + taken * j, c, taken),
            stats,
        )
    merged = []
    for top, sums, cross in stats:
        best = jnp.max(top, axis=0, keepdims=True)
        factor = jnp.exp(top - best)
        denom = jnp.sum(sums * factor, axis=0, keepdims=True)
        delta = jnp.sum(cross * factor, axis=0, keepdims=True) / denom
        merged.append((best + jnp.log(denom), delta))

    dqt_scr[...] = jnp.zeros_like(dqt_scr)

    def gradients(slot, taken):
        spots, ats = rows_of(slot, taken)
        for g in range(packs):
            log_total, delta = merged[g]
            cols = slice(g * PAIR, (g + 1) * PAIR)
            halves, grads = [], []
            for i in range(taken):
                weight = jnp.exp(s_scr[slot + i, g] - log_total)
                grads.append((weight * (p_scr[slot + i, g] - delta)).astype(jnp.bfloat16))
                halves.append(weight.astype(jnp.bfloat16))
            grad, half = joined(grads), joined(halves)
            dv = jnp.dot(half, do_bd[g], preferred_element_type=jnp.float32)
            dk = jnp.dot(grad, q_bd[g], preferred_element_type=jnp.float32)
            for i, at in enumerate(ats):
                acc_v[at, cols] += dv[i * BS : (i + 1) * BS]
                acc_k[at, cols] += dk[i * BS : (i + 1) * BS]
            for h in range(2):
                low = g * PAIR + h * HD
                kt = joined(
                    [kt_scr[pl.ds(pl.multiple_of(spot * feat + low, HD), HD), :] for spot in spots], 1
                )
                dqt_scr[low : low + HD, :] += jnp.dot(
                    kt, grad[:, h * BS : (h + 1) * BS], preferred_element_type=jnp.float32
                )

    for taken, first, count in groups:

        @pl.loop(0, count)
        def _(j):
            gradients(first + taken * j, taken)

    dq_ref[...] = (dqt_scr[...].T * SCALE).astype(jnp.bfloat16)

    @pl.when(step == steps - 1)
    def _():
        for i, acc in enumerate((acc_k, acc_v)):
            for side, base in enumerate((0, halo + rows)):

                @pl.loop(0, halo // BS)
                def _(b):
                    round_scr[i, side, pl.ds(b * BS, BS), :] = acc[
                        pl.ds(base + b * BS, BS), :
                    ].astype(jnp.bfloat16)

        copies = []
        for i, acc in enumerate((acc_k, acc_v)):
            copies += [
                pltpu.make_async_copy(acc.at[pl.ds(halo, rows)], own_ref.at[i], sems.at[3 * i]),
                pltpu.make_async_copy(round_scr.at[i, 0], left_ref.at[i], sems.at[3 * i + 1]),
                pltpu.make_async_copy(round_scr.at[i, 1], right_ref.at[i], sems.at[3 * i + 2]),
            ]
        for copy in copies:
            copy.start()
        for copy in copies:
            copy.wait()


def attend(spots, lengths, q, do, k, v):
    rows, feat = q.shape
    total = k.shape[0]
    halo = (total - rows) // 2
    packs = feat // PAIR
    slots = spots.shape[1]
    hbm = pl.BlockSpec(memory_space=pl.ANY)
    block = pl.BlockSpec((BS, feat), lambda i, *_: (i, 0))
    f32, bf16 = jnp.float32, jnp.bfloat16
    return pl.pallas_call(
        attend_kernel,
        grid_spec=pltpu.PrefetchScalarGridSpec(
            num_scalar_prefetch=2,
            grid=(rows // BS,),
            in_specs=[block, block] + [hbm] * 2,
            out_specs=[block, hbm, hbm, hbm],
            scratch_shapes=[
                pltpu.VMEM((total, feat), bf16),
                pltpu.VMEM((total, feat), bf16),
                pltpu.VMEM((total // BS * feat, BS), bf16),
                pltpu.VMEM((total, feat), f32),
                pltpu.VMEM((total, feat), f32),
                pltpu.VMEM((slots, packs, BS, 2 * BS), f32),
                pltpu.VMEM((slots, packs, BS, 2 * BS), f32),
                pltpu.VMEM((packs, 2 * BS, PAIR), bf16),
                pltpu.VMEM((packs, 2 * BS, PAIR), bf16),
                pltpu.VMEM((packs, PAIR, 2 * BS), bf16),
                pltpu.VMEM((packs, PAIR, 2 * BS), bf16),
                pltpu.VMEM((feat, BS), f32),
                pltpu.VMEM((2, 2, halo, feat), bf16),
                pltpu.SemaphoreType.DMA((6,)),
            ],
        ),
        out_shape=[
            jax.ShapeDtypeStruct((rows, feat), bf16),
            jax.ShapeDtypeStruct((2, rows, feat), f32),
            jax.ShapeDtypeStruct((2, halo, feat), bf16),
            jax.ShapeDtypeStruct((2, halo, feat), bf16),
        ],
        compiler_params=pltpu.CompilerParams(vmem_limit_bytes=60 * MIB),
        name="attend",
    )(spots, lengths, q, do, k, v)


def greet(n):
    me = lax.axis_index("uly")
    count = lax.axis_size("blk")
    rank = lax.axis_index("blk")
    left, right = lax.rem(rank + count - 1, count), lax.rem(rank + 1, count)
    barrier = pltpu.get_barrier_semaphore()
    for d in range(1, n):
        pl.semaphore_signal(barrier, 1, device_id={"uly": lax.rem(me + d, n)}, device_id_type=MESH)
    for side in (left, right):
        pl.semaphore_signal(barrier, 1, device_id={"blk": side}, device_id_type=MESH)
    pl.semaphore_wait(barrier, n + 1)
    return me, left, right


def remote(src, dst, send, recv, where):
    return pltpu.make_async_remote_copy(
        src_ref=src, dst_ref=dst, send_sem=send, recv_sem=recv, device_id=where, device_id_type=MESH
    )


def distances(n):
    return sorted(range(1, n), key=lambda d: -min(d, n - d))


def column_pieces(feat):
    return [slice(start, start + PAIR) for start in range(0, feat, PAIR)]


def spread_kernel(
    n, q_ref, k_ref, v_ref, do_ref, q_out, do_out, k_out, v_out,
    send_sem, recv_sem, own_sem, halo_send, halo_recv,
):
    me, left, right = greet(n)
    part = q_ref.shape[0]
    rows, feat = q_out.shape
    halo = (k_out.shape[0] - rows) // 2
    pieces = column_pieces(feat)
    whole = slice(0, feat)
    units = [(k_ref, k_out, halo, cols) for cols in pieces]
    units += [(v_ref, v_out, halo, cols) for cols in pieces]
    units += [(q_ref, q_out, 0, whole), (do_ref, do_out, 0, whole)]
    near = 2 * len(pieces)
    sent, kept = [], []
    for u, (src, dst, offset, cols) in enumerate(units):
        width = cols.stop - cols.start
        here = dst.at[pl.ds(pl.multiple_of(offset + me * part, BS), part), cols]
        mine = []
        for d in distances(n):
            peer = lax.rem(me + d, n)
            copy = remote(
                src.at[:, pl.ds(pl.multiple_of(peer * feat + cols.start, PAIR), width)], here,
                send_sem.at[u, d], recv_sem.at[u, d], {"uly": peer},
            )
            copy.start()
            mine.append(copy)
        sent.append(mine)
        copy = pltpu.make_async_copy(
            src.at[:, pl.ds(pl.multiple_of(me * feat + cols.start, PAIR), width)], here, own_sem.at[u]
        )
        copy.start()
        kept.append(copy)
    halos = []
    for u, (_, out, _, cols) in enumerate(units):
        kept[u].wait()
        for copy in sent[u]:
            copy.wait_recv()
        if u >= near:
            continue
        for i, (src, dst, side) in enumerate(((rows, 0, right), (halo, halo + rows, left))):
            copy = remote(
                out.at[pl.ds(src, halo), cols], out.at[pl.ds(dst, halo), cols],
                halo_send.at[u, i], halo_recv.at[u, i], {"blk": side},
            )
            copy.start()
            halos.append(copy)
    for mine in sent:
        for copy in mine:
            copy.wait_send()
    for copy in halos:
        copy.wait()


def spread(n, q, k, v, do):
    part, width = q.shape
    rows, feat = part * n, width // n
    halo = REACHB * BS
    hbm = pl.BlockSpec(memory_space=pl.ANY)
    flat = jax.ShapeDtypeStruct((rows, feat), q.dtype)
    wide = jax.ShapeDtypeStruct((rows + 2 * halo, feat), q.dtype)
    near = 2 * len(column_pieces(feat))
    return pl.pallas_call(
        functools.partial(spread_kernel, n),
        in_specs=[hbm] * 4,
        out_specs=[hbm] * 4,
        out_shape=[flat, flat, wide, wide],
        scratch_shapes=[
            pltpu.SemaphoreType.DMA((near + 2, n)),
            pltpu.SemaphoreType.DMA((near + 2, n)),
            pltpu.SemaphoreType.DMA((near + 2,)),
            pltpu.SemaphoreType.DMA((near, 2)),
            pltpu.SemaphoreType.DMA((near, 2)),
        ],
        compiler_params=pltpu.CompilerParams(collective_id=0, has_side_effects=True),
        name="spread",
    )(q, k, v, do)


def collect_kernel(
    n, dq_ref, own_ref, left_ref, right_ref, dq_out, dk_out, dv_out,
    own_scr, res_scr, from_left, from_right,
    send_sem, recv_sem, own_sem, load_sem, halo_send, halo_recv,
):
    me, left, right = greet(n)
    _, rows, feat = own_ref.shape
    halo = left_ref.shape[1]
    part = rows // n
    units = [(a, cols) for a in range(2) for cols in column_pieces(feat)]
    halos = []
    for u, (a, cols) in enumerate(units):
        pair = (
            remote(
                left_ref.at[a, :, cols], from_right.at[a, :, cols],
                halo_send.at[u, 0], halo_recv.at[u, 0], {"blk": left},
            ),
            remote(
                right_ref.at[a, :, cols], from_left.at[a, :, cols],
                halo_send.at[u, 1], halo_recv.at[u, 1], {"blk": right},
            ),
        )
        for copy in pair:
            copy.start()
        halos.append(pair)
    loads = [pltpu.make_async_copy(own_ref.at[a], own_scr.at[a], load_sem.at[a]) for a in range(2)]
    for load in loads:
        load.start()
    pending, kept = [], []

    def send(u, rows_from, out, start, width):
        there = out.at[:, pl.ds(pl.multiple_of(me * feat + start, PAIR), width)]
        for d in distances(n):
            peer = lax.rem(me + d, n)
            copy = remote(
                rows_from(pl.ds(pl.multiple_of(peer * part, BS), part)), there,
                send_sem.at[u, d], recv_sem.at[u, d], {"uly": peer},
            )
            copy.start()
            pending.append(copy)
        copy = pltpu.make_async_copy(
            rows_from(pl.ds(pl.multiple_of(me * part, BS), part)), there, own_sem.at[u]
        )
        copy.start()
        kept.append(copy)

    send(len(units), lambda at: dq_ref.at[at], dq_out, 0, feat)
    for a in range(2):
        loads[a].wait()

        @pl.loop(halo // BS, (rows - halo) // BS)
        def _(t):
            at = pl.ds(pl.multiple_of(t * BS, BS), BS)
            res_scr[a, at, :] = own_scr[a, at, :].astype(jnp.bfloat16)

    for u, (a, cols) in enumerate(units):
        for copy in halos[u]:
            copy.wait_recv()

        @pl.loop(0, halo // BS)
        def _(t):
            for base, arrived in ((0, from_left), (rows - halo, from_right)):
                at = pl.ds(pl.multiple_of(base + t * BS, BS), BS)
                more = arrived[a, pl.ds(pl.multiple_of(t * BS, BS), BS), cols].astype(jnp.float32)
                res_scr[a, at, cols] = (own_scr[a, at, cols] + more).astype(jnp.bfloat16)

        send(
            u, lambda at: res_scr.at[a, at, cols], (dk_out, dv_out)[a],
            cols.start, cols.stop - cols.start,
        )
    for copy in kept:
        copy.wait()
    for copy in pending:
        copy.wait()
    for pair in halos:
        for copy in pair:
            copy.wait_send()


def collect(n, dq, own, left, right):
    rows, feat = dq.shape
    halo = left.shape[1]
    near = 2 * len(column_pieces(feat))
    bf16 = jnp.bfloat16
    hbm = pl.BlockSpec(memory_space=pl.ANY)
    return pl.pallas_call(
        functools.partial(collect_kernel, n),
        in_specs=[hbm] * 4,
        out_specs=[hbm] * 3,
        out_shape=[jax.ShapeDtypeStruct((rows // n, feat * n), bf16)] * 3,
        scratch_shapes=[
            pltpu.VMEM((2, rows, feat), jnp.float32),
            pltpu.VMEM((2, rows, feat), bf16),
            pltpu.VMEM((2, halo, feat), bf16),
            pltpu.VMEM((2, halo, feat), bf16),
            pltpu.SemaphoreType.DMA((near + 1, n)),
            pltpu.SemaphoreType.DMA((near + 1, n)),
            pltpu.SemaphoreType.DMA((near + 1,)),
            pltpu.SemaphoreType.DMA((2,)),
            pltpu.SemaphoreType.DMA((near, 2)),
            pltpu.SemaphoreType.DMA((near, 2)),
        ],
        compiler_params=pltpu.CompilerParams(
            collective_id=1, has_side_effects=True, vmem_limit_bytes=60 * MIB
        ),
        name="collect",
    )(dq, own, left, right)


def local_lists(key_lists, list_length, per_rank):
    block_rank = lax.axis_index("blk")
    all_blocks = per_rank * lax.axis_size("blk")
    base_block = block_rank * per_rank - REACHB
    lists_here = lax.dynamic_slice_in_dim(key_lists, block_rank * per_rank, per_rank, 0)
    lengths_here = lax.dynamic_slice_in_dim(list_length, block_rank * per_rank, per_rank, 0)
    return (lists_here - base_block) % all_blocks, lengths_here


def shards(queries, keys, values, grad_out, key_lists, list_length):
    n = lax.axis_size("uly")
    q, do, k, v = spread(n, queries, keys, values, grad_out)
    spots, lengths = local_lists(key_lists, list_length, q.shape[0] // BS)
    dq, own, left, right = attend(spots, lengths, q, do, k, v)
    return tuple(collect(n, dq, own, left, right))


def solution(mesh):
    rows = P(("grp", "blk", "uly"), None)
    return jax.shard_map(
        shards,
        mesh=mesh,
        in_specs=(rows, rows, rows, rows, P("grp", None), P("grp")),
        out_specs=(rows, rows, rows),
        check_vma=False,
    )
```

```python
import functools

import jax
import jax.numpy as jnp
from jax import lax
from jax.experimental import pallas as pl
from jax.experimental.pallas import tpu as pltpu
from jax.sharding import PartitionSpec as P

HD = 64
BS = 128
REACHB = 6
PAIR = 2 * HD
SCALE = HD ** (-0.5)
GROUPS = (4, 2, 1)
MIB = 1024 * 1024
MESH = pl.DeviceIdType.MESH


def block_diagonal(pair, factor):
    wide = pair.astype(jnp.float32) * factor
    lane = lax.broadcasted_iota(jnp.int32, wide.shape, 1)
    first = jnp.where(lane < HD, wide, 0.0).astype(jnp.bfloat16)
    second = jnp.where(lane < HD, 0.0, wide).astype(jnp.bfloat16)
    return first, second


def attend_kernel(
    spots_ref, lengths_ref, q_ref, do_ref, k_ref, v_ref,
    dq_ref, own_ref, left_ref, right_ref,
    k_scr, v_scr, kt_scr, acc_k, acc_v, s_scr, p_scr, q_bd, do_bd, q_bdt, do_bdt, dqt_scr, round_scr, sems,
):
    step = pl.program_id(0)
    steps = pl.num_programs(0)
    halo = left_ref.shape[1]
    total, feat = k_scr.shape
    rows = total - 2 * halo
    packs = feat // PAIR

    @pl.when(step == 0)
    def _():
        copies = [
            pltpu.make_async_copy(k_ref, k_scr, sems.at[0]),
            pltpu.make_async_copy(v_ref, v_scr, sems.at[1]),
        ]
        for copy in copies:
            copy.start()

        @pl.loop(0, total // BS)
        def _(b):
            at = pl.ds(b * BS, BS)
            acc_k[at, :] = jnp.zeros((BS, feat), jnp.float32)
            acc_v[at, :] = jnp.zeros((BS, feat), jnp.float32)

        copies[0].wait()

        @pl.loop(0, total // BS, unroll=4)
        def _(b):
            kt_scr[pl.ds(b * feat, feat), :] = k_scr[pl.ds(b * BS, BS), :].T

        copies[1].wait()

    for g in range(packs):
        cols = slice(g * PAIR, (g + 1) * PAIR)
        first, second = block_diagonal(q_ref[:, cols], SCALE)
        q_bd[g, :BS, :] = first
        q_bd[g, BS:, :] = second
        first, second = block_diagonal(do_ref[:, cols], 1.0)
        do_bd[g, :BS, :] = first
        do_bd[g, BS:, :] = second
        q_bdt[g] = q_bd[g].T
        do_bdt[g] = do_bd[g].T

    length = lengths_ref[step]
    groups, done = [], 0
    for taken in GROUPS:
        count = (length - done) // taken
        groups.append((taken, done, count))
        done = done + taken * count

    def rows_of(slot, taken):
        spots = [spots_ref[step, slot + i] for i in range(taken)]
        return spots, [pl.ds(pl.multiple_of(spot * BS, BS), BS) for spot in spots]

    def joined(pieces, axis=0):
        return pieces[0] if len(pieces) == 1 else jnp.concatenate(pieces, axis=axis)

    def scores(slot, carry, taken):
        _, ats = rows_of(slot, taken)
        out = []
        for g in range(packs):
            top, sums, cross = carry[g]
            cols = slice(g * PAIR, (g + 1) * PAIR)
            keys = joined([k_scr[at, cols] for at in ats])
            values = joined([v_scr[at, cols] for at in ats])
            s = jnp.dot(keys, q_bdt[g], preferred_element_type=jnp.float32)
            dp = jnp.dot(values, do_bdt[g], preferred_element_type=jnp.float32)
            for i in range(taken):
                s_scr[slot + i, g] = s[i * BS : (i + 1) * BS]
                p_scr[slot + i, g] = dp[i * BS : (i + 1) * BS]
            s = s.reshape(taken * BS // 8, 8, 2 * BS)
            dp = dp.reshape(taken * BS // 8, 8, 2 * BS)
            new_top = jnp.maximum(top, jnp.max(s, axis=0))
            keep = jnp.exp(top - new_top)
            p = jnp.exp(s - new_top[None])
            out.append(
                (
                    new_top,
                    sums * keep + jnp.sum(p, axis=0),
                    cross * keep + jnp.sum(p * dp, axis=0),
                )
            )
        return tuple(out)

    blank = jnp.zeros((8, 2 * BS), jnp.float32)
    start = tuple((blank - jnp.inf, blank, blank) for _ in range(packs))
    stats = start
    for taken, first, count in groups:
        stats = lax.fori_loop(
            0,
            count,
            lambda j, c, taken=taken, first=first: scores(first + taken * j, c, taken),
            stats,
        )
    merged = []
    for top, sums, cross in stats:
        best = jnp.max(top, axis=0, keepdims=True)
        factor = jnp.exp(top - best)
        denom = jnp.sum(sums * factor, axis=0, keepdims=True)
        delta = jnp.sum(cross * factor, axis=0, keepdims=True) / denom
        merged.append((best + jnp.log(denom), delta))

    dqt_scr[...] = jnp.zeros_like(dqt_scr)

    def gradients(slot, taken):
        spots, ats = rows_of(slot, taken)
        for g in range(packs):
            log_total, delta = merged[g]
            cols = slice(g * PAIR, (g + 1) * PAIR)
            halves, grads = [], []
            for i in range(taken):
                weight = jnp.exp(s_scr[slot + i, g] - log_total)
                grads.append((weight * (p_scr[slot + i, g] - delta)).astype(jnp.bfloat16))
                halves.append(weight.astype(jnp.bfloat16))
            grad, half = joined(grads), joined(halves)
            dv = jnp.dot(half, do_bd[g], preferred_element_type=jnp.float32)
            dk = jnp.dot(grad, q_bd[g], preferred_element_type=jnp.float32)
            for i, at in enumerate(ats):
                acc_v[at, cols] += dv[i * BS : (i + 1) * BS]
                acc_k[at, cols] += dk[i * BS : (i + 1) * BS]
            for h in range(2):
                low = g * PAIR + h * HD
                kt = joined(
                    [kt_scr[pl.ds(pl.multiple_of(spot * feat + low, HD), HD), :] for spot in spots], 1
                )
                dqt_scr[low : low + HD, :] += jnp.dot(
                    kt, grad[:, h * BS : (h + 1) * BS], preferred_element_type=jnp.float32
                )

    for taken, first, count in groups:

        @pl.loop(0, count)
        def _(j):
            gradients(first + taken * j, taken)

    dq_ref[...] = (dqt_scr[...].T * SCALE).astype(jnp.bfloat16)

    @pl.when(step == steps - 1)
    def _():
        copies = []

        def begin(src, dst):
            copy = pltpu.make_async_copy(src, dst, sems.at[len(copies)])
            copy.start()
            copies.append(copy)

        for i, acc in enumerate((acc_k, acc_v)):
            begin(acc.at[pl.ds(halo, rows)], own_ref.at[i])
        for i, acc in enumerate((acc_k, acc_v)):
            for side, (base, out) in enumerate(((0, left_ref), (halo + rows, right_ref))):

                @pl.loop(0, halo // BS, unroll=2)
                def _(b):
                    round_scr[i, side, pl.ds(b * BS, BS), :] = acc[
                        pl.ds(base + b * BS, BS), :
                    ].astype(jnp.bfloat16)

                begin(round_scr.at[i, side], out.at[i])
        for copy in copies:
            copy.wait()


def attend(spots, lengths, q, do, k, v):
    rows, feat = q.shape
    total = k.shape[0]
    halo = (total - rows) // 2
    packs = feat // PAIR
    slots = spots.shape[1]
    hbm = pl.BlockSpec(memory_space=pl.ANY)
    block = pl.BlockSpec((BS, feat), lambda i, *_: (i, 0))
    f32, bf16 = jnp.float32, jnp.bfloat16
    return pl.pallas_call(
        attend_kernel,
        grid_spec=pltpu.PrefetchScalarGridSpec(
            num_scalar_prefetch=2,
            grid=(rows // BS,),
            in_specs=[block, block] + [hbm] * 2,
            out_specs=[block, hbm, hbm, hbm],
            scratch_shapes=[
                pltpu.VMEM((total, feat), bf16),
                pltpu.VMEM((total, feat), bf16),
                pltpu.VMEM((total // BS * feat, BS), bf16),
                pltpu.VMEM((total, feat), f32),
                pltpu.VMEM((total, feat), f32),
                pltpu.VMEM((slots, packs, BS, 2 * BS), f32),
                pltpu.VMEM((slots, packs, BS, 2 * BS), f32),
                pltpu.VMEM((packs, 2 * BS, PAIR), bf16),
                pltpu.VMEM((packs, 2 * BS, PAIR), bf16),
                pltpu.VMEM((packs, PAIR, 2 * BS), bf16),
                pltpu.VMEM((packs, PAIR, 2 * BS), bf16),
                pltpu.VMEM((feat, BS), f32),
                pltpu.VMEM((2, 2, halo, feat), bf16),
                pltpu.SemaphoreType.DMA((6,)),
            ],
        ),
        out_shape=[
            jax.ShapeDtypeStruct((rows, feat), bf16),
            jax.ShapeDtypeStruct((2, rows, feat), f32),
            jax.ShapeDtypeStruct((2, halo, feat), bf16),
            jax.ShapeDtypeStruct((2, halo, feat), bf16),
        ],
        compiler_params=pltpu.CompilerParams(vmem_limit_bytes=60 * MIB),
        name="attend",
    )(spots, lengths, q, do, k, v)


def greet(n):
    me = lax.axis_index("uly")
    count = lax.axis_size("blk")
    rank = lax.axis_index("blk")
    left, right = lax.rem(rank + count - 1, count), lax.rem(rank + 1, count)
    barrier = pltpu.get_barrier_semaphore()
    for d in range(1, n):
        pl.semaphore_signal(barrier, 1, device_id={"uly": lax.rem(me + d, n)}, device_id_type=MESH)
    for side in (left, right):
        pl.semaphore_signal(barrier, 1, device_id={"blk": side}, device_id_type=MESH)
    pl.semaphore_wait(barrier, n + 1)
    return me, left, right


def remote(src, dst, send, recv, where):
    return pltpu.make_async_remote_copy(
        src_ref=src, dst_ref=dst, send_sem=send, recv_sem=recv, device_id=where, device_id_type=MESH
    )


def distances(n):
    return sorted(range(1, n), key=lambda d: -min(d, n - d))


def column_pieces(feat):
    return [slice(start, start + PAIR) for start in range(0, feat, PAIR)]


def spread_kernel(
    n, q_ref, k_ref, v_ref, do_ref, q_out, do_out, k_out, v_out,
    send_sem, recv_sem, own_sem, halo_send, halo_recv,
):
    me, left, right = greet(n)
    part = q_ref.shape[0]
    rows, feat = q_out.shape
    halo = (k_out.shape[0] - rows) // 2
    pieces = column_pieces(feat)
    whole = slice(0, feat)
    units = [(k_ref, k_out, halo, cols) for cols in pieces]
    units += [(v_ref, v_out, halo, cols) for cols in pieces]
    units += [(q_ref, q_out, 0, whole), (do_ref, do_out, 0, whole)]
    near = 2 * len(pieces)
    sent, kept = [], []
    for u, (src, dst, offset, cols) in enumerate(units):
        width = cols.stop - cols.start
        here = dst.at[pl.ds(pl.multiple_of(offset + me * part, BS), part), cols]
        mine = []
        for d in distances(n):
            peer = lax.rem(me + d, n)
            copy = remote(
                src.at[:, pl.ds(pl.multiple_of(peer * feat + cols.start, PAIR), width)], here,
                send_sem.at[u, d], recv_sem.at[u, d], {"uly": peer},
            )
            copy.start()
            mine.append(copy)
        sent.append(mine)
        copy = pltpu.make_async_copy(
            src.at[:, pl.ds(pl.multiple_of(me * feat + cols.start, PAIR), width)], here, own_sem.at[u]
        )
        copy.start()
        kept.append(copy)
    halos = []
    for u, (_, out, _, cols) in enumerate(units):
        kept[u].wait()
        for copy in sent[u]:
            copy.wait_recv()
        if u >= near:
            continue
        for i, (src, dst, side) in enumerate(((rows, 0, right), (halo, halo + rows, left))):
            copy = remote(
                out.at[pl.ds(src, halo), cols], out.at[pl.ds(dst, halo), cols],
                halo_send.at[u, i], halo_recv.at[u, i], {"blk": side},
            )
            copy.start()
            halos.append(copy)
    for mine in sent:
        for copy in mine:
            copy.wait_send()
    for copy in halos:
        copy.wait()


def spread(n, q, k, v, do):
    part, width = q.shape
    rows, feat = part * n, width // n
    halo = REACHB * BS
    hbm = pl.BlockSpec(memory_space=pl.ANY)
    flat = jax.ShapeDtypeStruct((rows, feat), q.dtype)
    wide = jax.ShapeDtypeStruct((rows + 2 * halo, feat), q.dtype)
    near = 2 * len(column_pieces(feat))
    return pl.pallas_call(
        functools.partial(spread_kernel, n),
        in_specs=[hbm] * 4,
        out_specs=[hbm] * 4,
        out_shape=[flat, flat, wide, wide],
        scratch_shapes=[
            pltpu.SemaphoreType.DMA((near + 2, n)),
            pltpu.SemaphoreType.DMA((near + 2, n)),
            pltpu.SemaphoreType.DMA((near + 2,)),
            pltpu.SemaphoreType.DMA((near, 2)),
            pltpu.SemaphoreType.DMA((near, 2)),
        ],
        compiler_params=pltpu.CompilerParams(collective_id=0, has_side_effects=True),
        name="spread",
    )(q, k, v, do)


def collect_kernel(
    n, dq_ref, own_ref, left_ref, right_ref, dq_out, dk_out, dv_out,
    own_scr, res_scr, from_left, from_right,
    send_sem, recv_sem, own_sem, load_sem, halo_send, halo_recv,
):
    me, left, right = greet(n)
    _, rows, feat = own_ref.shape
    halo = left_ref.shape[1]
    part = rows // n
    units = [(a, cols) for a in range(2) for cols in column_pieces(feat)]
    halos = []
    for u, (a, cols) in enumerate(units):
        pair = (
            remote(
                left_ref.at[a, :, cols], from_right.at[a, :, cols],
                halo_send.at[u, 0], halo_recv.at[u, 0], {"blk": left},
            ),
            remote(
                right_ref.at[a, :, cols], from_left.at[a, :, cols],
                halo_send.at[u, 1], halo_recv.at[u, 1], {"blk": right},
            ),
        )
        for copy in pair:
            copy.start()
        halos.append(pair)
    loads = [pltpu.make_async_copy(own_ref.at[a], own_scr.at[a], load_sem.at[a]) for a in range(2)]
    for load in loads:
        load.start()
    pending, kept = [], []

    def send(u, rows_from, out, start, width):
        there = out.at[:, pl.ds(pl.multiple_of(me * feat + start, PAIR), width)]
        for d in distances(n):
            peer = lax.rem(me + d, n)
            copy = remote(
                rows_from(pl.ds(pl.multiple_of(peer * part, BS), part)), there,
                send_sem.at[u, d], recv_sem.at[u, d], {"uly": peer},
            )
            copy.start()
            pending.append(copy)
        copy = pltpu.make_async_copy(
            rows_from(pl.ds(pl.multiple_of(me * part, BS), part)), there, own_sem.at[u]
        )
        copy.start()
        kept.append(copy)

    send(len(units), lambda at: dq_ref.at[at], dq_out, 0, feat)
    for a in range(2):
        loads[a].wait()

        @pl.loop(halo // BS, (rows - halo) // BS)
        def _(t):
            at = pl.ds(pl.multiple_of(t * BS, BS), BS)
            res_scr[a, at, :] = own_scr[a, at, :].astype(jnp.bfloat16)

    for u, (a, cols) in enumerate(units):
        for copy in halos[u]:
            copy.wait_recv()

        @pl.loop(0, halo // BS)
        def _(t):
            for base, arrived in ((0, from_left), (rows - halo, from_right)):
                at = pl.ds(pl.multiple_of(base + t * BS, BS), BS)
                more = arrived[a, pl.ds(pl.multiple_of(t * BS, BS), BS), cols].astype(jnp.float32)
                res_scr[a, at, cols] = (own_scr[a, at, cols] + more).astype(jnp.bfloat16)

        send(
            u, lambda at: res_scr.at[a, at, cols], (dk_out, dv_out)[a],
            cols.start, cols.stop - cols.start,
        )
    for copy in kept:
        copy.wait()
    for copy in pending:
        copy.wait()
    for pair in halos:
        for copy in pair:
            copy.wait_send()


def collect(n, dq, own, left, right):
    rows, feat = dq.shape
    halo = left.shape[1]
    near = 2 * len(column_pieces(feat))
    bf16 = jnp.bfloat16
    hbm = pl.BlockSpec(memory_space=pl.ANY)
    return pl.pallas_call(
        functools.partial(collect_kernel, n),
        in_specs=[hbm] * 4,
        out_specs=[hbm] * 3,
        out_shape=[jax.ShapeDtypeStruct((rows // n, feat * n), bf16)] * 3,
        scratch_shapes=[
            pltpu.VMEM((2, rows, feat), jnp.float32),
            pltpu.VMEM((2, rows, feat), bf16),
            pltpu.VMEM((2, halo, feat), bf16),
            pltpu.VMEM((2, halo, feat), bf16),
            pltpu.SemaphoreType.DMA((near + 1, n)),
            pltpu.SemaphoreType.DMA((near + 1, n)),
            pltpu.SemaphoreType.DMA((near + 1,)),
            pltpu.SemaphoreType.DMA((2,)),
            pltpu.SemaphoreType.DMA((near, 2)),
            pltpu.SemaphoreType.DMA((near, 2)),
        ],
        compiler_params=pltpu.CompilerParams(
            collective_id=1, has_side_effects=True, vmem_limit_bytes=60 * MIB
        ),
        name="collect",
    )(dq, own, left, right)


def local_lists(key_lists, list_length, per_rank):
    block_rank = lax.axis_index("blk")
    all_blocks = per_rank * lax.axis_size("blk")
    base_block = block_rank * per_rank - REACHB
    lists_here = lax.dynamic_slice_in_dim(key_lists, block_rank * per_rank, per_rank, 0)
    lengths_here = lax.dynamic_slice_in_dim(list_length, block_rank * per_rank, per_rank, 0)
    return (lists_here - base_block) % all_blocks, lengths_here


def shards(queries, keys, values, grad_out, key_lists, list_length):
    n = lax.axis_size("uly")
    q, do, k, v = spread(n, queries, keys, values, grad_out)
    spots, lengths = local_lists(key_lists, list_length, q.shape[0] // BS)
    dq, own, left, right = attend(spots, lengths, q, do, k, v)
    return tuple(collect(n, dq, own, left, right))


def solution(mesh):
    rows = P(("grp", "blk", "uly"), None)
    return jax.shard_map(
        shards,
        mesh=mesh,
        in_specs=(rows, rows, rows, rows, P("grp", None), P("grp")),
        out_specs=(rows, rows, rows),
        check_vma=False,
    )
```
